32 devices in a mesh: dp: 4 (over x, core), fsdp: 8 (over z, y).
Axes of the slice: x: 2, y: 2, z: 4, core: 2. Of those that a mesh axis runs over, the one named last changes fastest.
Arguments:
- inputs: bfloat16 [16, 1024, 768], P('dp', 'fsdp'), may hold values from -6 to 6
- segments: int32 [16, 1024], P('dp', 'fsdp'), may hold values from 0 to 3, as said below
- cotangent: bfloat16 [16, 1024, 768], P('dp', 'fsdp'), may hold values from -6 to 6
- qkv_weight: bfloat16 [768, 2304], P('fsdp'), may hold values from -0.21875 to 0.21875
- query_bias: bfloat16 [768], P('fsdp'), may hold values from -3 to 3
- value_bias: bfloat16 [768], P('fsdp'), may hold values from -3 to 3
- out_weight: bfloat16 [768, 768], P('fsdp'), may hold values from -0.875 to 0.875
- out_bias: bfloat16 [768], P('fsdp'), may hold values from -1.75 to 1.75
- norm1_gain: bfloat16 [768], P('fsdp'), may hold values from 0.099609375 to 1.8984375
- norm1_shift: bfloat16 [768], P('fsdp'), may hold values from -3 to 3
- up_weight: bfloat16 [768, 3072], P('fsdp'), may hold values from -0.21875 to 0.21875
- up_bias: bfloat16 [3072], P('fsdp'), may hold values from -3 to 3
- down_weight: bfloat16 [3072, 768], P('fsdp'), may hold values from -0.109375 to 0.109375
- down_bias: bfloat16 [768], P('fsdp'), may hold values from -1.75 to 1.75
- norm2_gain: bfloat16 [768], P('fsdp'), may hold values from 0.099609375 to 1.8984375
- norm2_shift: bfloat16 [768], P('fsdp'), may hold values from -3 to 3
Outputs:
- output: bfloat16 [16, 1024, 768], P('dp', 'fsdp')
- d_inputs: bfloat16 [16, 1024, 768], P('dp', 'fsdp')
- d_qkv_weight: float32 [768, 2304], P('fsdp')
- d_query_bias: float32 [768], P('fsdp')
- d_value_bias: float32 [768], P('fsdp')
- d_out_weight: float32 [768, 768], P('fsdp')
- d_out_bias: float32 [768], P('fsdp')
- d_norm1_gain: float32 [768], P('fsdp')
- d_norm1_shift: float32 [768], P('fsdp')
- d_up_weight: float32 [768, 3072], P('fsdp')
- d_up_bias: float32 [3072], P('fsdp')
- d_down_weight: float32 [3072, 768], P('fsdp')
- d_down_bias: float32 [768], P('fsdp')
- d_norm2_gain: float32 [768], P('fsdp')
- d_norm2_shift: float32 [768], P('fsdp')
The draws below stay inside these ranges and needn't reach their ends.
Inputs may be any that keep to these rules, and one draw needn't show every extreme that they name: `segments`: within each sequence the numbers start at 0 and never fall; in each group of 4 consecutive sequences one sequence is a single document.
All inputs are finite; a program needn't handle non-finite values.
Results may differ from the reference program's by a relative error of at most 0.02.
Values may be sent and summed in bfloat16 or wider, within the bound.
No kernel may reach another device: no remote copies, remote signals or barrier semaphores. Data moves between devices by JAX's collectives and lax.ppermute only.
A program may use at most 384 MiB of HBM per device.

```python
import jax
import jax.numpy as jnp
from jax import lax

D = 768
FF = 3072
HEADS = 12
HEAD_DIM = 64
SEQS = 4
LENGTH = 1024
SEQUENCES = 16


def draw_segments(key, part):
    key = jax.random.fold_in(key, 7)
    key_cuts, key_pick = jax.random.split(key)
    cuts = jnp.sort(jax.random.randint(key_cuts, (SEQUENCES, 3), 1, LENGTH), axis=1)
    groups = SEQUENCES // SEQS
    picked = jax.random.randint(key_pick, (groups, 1), 0, SEQS)
    within = jnp.arange(SEQS, dtype=jnp.int32)[None, :]
    single = (within == picked).reshape(SEQUENCES)
    cuts = jnp.where(single[:, None], LENGTH, cuts)
    positions = jnp.arange(LENGTH, dtype=jnp.int32)
    passed = positions[None, :, None] >= cuts[:, None, :]
    return jnp.sum(passed.astype(jnp.int32), axis=2).astype(jnp.int32)


def levels(rng, dims, cuts, smallest, largest):
    def one(position, blocks):
        steps = jax.random.uniform(jax.random.fold_in(jax.random.fold_in(rng, 6), position), (blocks,), jnp.float32, smallest / len(cuts), largest / len(cuts))
        return jnp.repeat(jnp.exp(steps), dims[position] // blocks).reshape((-1,) + (1,) * (len(dims) - position - 1))

    loudness = one(*cuts[0])
    for cut in cuts[1:]:
        loudness = loudness * one(*cut)
    return loudness


def gaussian(own_key, dims, scale, limit, shards=(), kind=jnp.bfloat16):
    factor_of = levels(own_key, dims, shards, -0.22, 0.18) if shards else 1.0
    array = jax.random.normal(own_key, dims, jnp.float32) * scale * factor_of
    return jnp.minimum(jnp.maximum(array, -limit), limit).astype(kind)


def setup_inputs(seed: int = 0) -> dict:
    streams_of = jax.random.split(jax.random.key(seed), 17)
    return {
        "inputs": gaussian(streams_of[0], (SEQUENCES, LENGTH, D), 1.0, 6.0, ((0, 4), (1, 8))),
        "segments": draw_segments(jax.random.fold_in(streams_of[16], 71), 0),
        "cotangent": gaussian(streams_of[2], (SEQUENCES, LENGTH, D), 1.0, 6.0, ((0, 4), (1, 8))),
        "qkv_weight": gaussian(streams_of[3], (D, 3 * D), D ** -0.5, 0.21875, ((0, 8),)),
        "query_bias": gaussian(streams_of[4], (D,), 0.5, 3.0, ((0, 8),)),
        "value_bias": gaussian(streams_of[5], (D,), 0.5, 3.0, ((0, 8),)),
        "out_weight": gaussian(streams_of[6], (D, D), (D // 16) ** -0.5, 0.875, ((0, 8),)),
        "out_bias": gaussian(streams_of[7], (D,), 0.3, 1.75, ((0, 8),)),
        "norm1_gain": jnp.clip(1.0 + 0.18 * jax.random.normal(streams_of[8], (D,), jnp.float32), 0.099609375, 1.8984375).astype(jnp.bfloat16),
        "norm1_shift": gaussian(streams_of[9], (D,), 0.5, 3.0, ((0, 8),)),
        "up_weight": gaussian(streams_of[10], (D, FF), D ** -0.5, 0.21875, ((0, 8),)),
        "up_bias": gaussian(streams_of[11], (FF,), 0.5, 3.0, ((0, 8),)),
        "down_weight": gaussian(streams_of[12], (FF, D), FF ** -0.5, 0.109375, ((0, 8),)),
        "down_bias": gaussian(streams_of[13], (D,), 0.3, 1.75, ((0, 8),)),
        "norm2_gain": jnp.clip(1.0 + 0.18 * jax.random.normal(streams_of[14], (D,), jnp.float32), 0.099609375, 1.8984375).astype(jnp.bfloat16),
        "norm2_shift": gaussian(streams_of[15], (D,), 0.5, 3.0, ((0, 8),)),
    }


@jax.custom_vjp
def low(v):
    return lax.optimization_barrier(v.astype(jnp.bfloat16)).astype(jnp.float32)

@jax.custom_vjp
def low_back(v):
    return v

def low_keep(v):
    return (low(v), None)

def low_pass(kept, grad):
    return (grad,)

def back_keep(v):
    return (v, None)

def back_low(kept, grad):
    return (low(grad),)
low.defvjp(low_keep, low_pass)
low_back.defvjp(back_keep, back_low)
HIGH = lax.Precision.HIGHEST

def both_ways(values):
    return low_back(low(values))

def matmul(left, right):
    return jnp.dot(left, right, precision=HIGH)

def layer_normalize(values, norm_gain, norm_shift):
    centered_input = values - lax.optimization_barrier(jnp.mean(values, axis=-1, keepdims=True))
    spread = lax.optimization_barrier(jnp.mean(centered_input * centered_input, axis=-1, keepdims=True))
    return centered_input * lax.rsqrt(spread + 1e-05) * norm_gain + norm_shift

def attention(queries, keys, values, segment):
    length = queries.shape[0]
    rows = min(512, length)
    count = length // rows
    scale = HEAD_DIM ** (-0.5)
    query_heads = queries.reshape(count, rows, HEADS, HEAD_DIM)
    key_heads = keys.reshape(length, HEADS, HEAD_DIM)
    value_heads = values.reshape(length, HEADS, HEAD_DIM)
    positions = jnp.arange(length, dtype=jnp.int32)
    starts = (jnp.arange(count, dtype=jnp.int32) * rows).astype(jnp.int32)

    def block_fn(item):
        query_block, start = item
        scores = low_back(jnp.einsum('qhd,khd->hqk', query_block, key_heads, precision=HIGH) * scale)
        query_pos = start + jnp.arange(rows, dtype=jnp.int32)
        query_seg = lax.dynamic_slice_in_dim(segment, start, rows)
        allowed = (positions[None, :] <= query_pos[:, None]) & (segment[None, :] == query_seg[:, None])
        scores = jnp.where(allowed[None], scores, jnp.float32(-1e+30))
        top = lax.optimization_barrier(jnp.max(scores, axis=-1, keepdims=True))
        expo = jnp.exp(scores - top)
        probs = expo / lax.optimization_barrier(jnp.sum(expo, axis=-1, keepdims=True))
        mixed = jnp.einsum('hqk,khd->qhd', low(probs), value_heads, precision=HIGH)
        return mixed.reshape(rows, HEADS * HEAD_DIM)
    blocks = lax.map(jax.checkpoint(block_fn), (query_heads, starts))
    return blocks.reshape(length, HEADS * HEAD_DIM)

def layer(inputs, segment, params):
    qkv_weight, query_bias, value_bias, out_weight, out_bias, norm1_gain, norm1_shift, up_weight, up_bias, down_weight, down_bias, norm2_gain, norm2_shift = params
    width = inputs.shape[1]
    hidden1 = low(layer_normalize(inputs, norm1_gain, norm1_shift))
    joined = matmul(hidden1, qkv_weight)
    queries = both_ways(joined[:, :width] + query_bias)
    keys = both_ways(joined[:, width:2 * width])
    values = both_ways(joined[:, 2 * width:] + value_bias)
    mixed = both_ways(attention(queries, keys, values, segment))
    branch = low_back(matmul(mixed, out_weight) + out_bias)
    midway_state = inputs + branch
    hidden2 = low(layer_normalize(midway_state, norm2_gain, norm2_shift))
    pre_act = low_back(matmul(hidden2, up_weight) + up_bias)
    activ = low(jax.nn.gelu(pre_act, approximate=True))
    return midway_state + matmul(activ, down_weight) + down_bias

def reference(inputs, segments, cotangent, qkv_weight, query_bias, value_bias, out_weight, out_bias, norm1_gain, norm1_shift, up_weight, up_bias, down_weight, down_bias, norm2_gain, norm2_shift):
    params = tuple((w.astype(jnp.float32) for w in (qkv_weight, query_bias, value_bias, out_weight, out_bias, norm1_gain, norm1_shift, up_weight, up_bias, down_weight, down_bias, norm2_gain, norm2_shift)))
    zeros = tuple((jnp.zeros_like(w) for w in params))

    def step(carry, item):
        sequence, segment, grad_out = item
        result, pull = jax.vjp(lambda values, weights: layer(values, segment, weights), sequence.astype(jnp.float32), params)
        d_seq, d_params = pull(grad_out.astype(jnp.float32))
        carry = jax.tree.map(lambda left, right: left + right, carry, d_params)
        return (carry, (result.astype(jnp.bfloat16), d_seq.astype(jnp.bfloat16)))
    grads, (output, d_inputs) = lax.scan(step, zeros, (inputs, segments, cotangent))
    return (output, d_inputs) + tuple(grads)
```

```python
import jax
import jax.numpy as jnp
from jax import lax
from jax.experimental import pallas as pl
from jax.experimental.pallas import tpu as pltpu
from jax.sharding import PartitionSpec as P

HEAD_DIM = 64
NEG = -1e30
f32 = jnp.float32
bf16 = jnp.bfloat16


def dot(a, b, ca, cb):
    return lax.dot_general(a, b, (((ca,), (cb,)), ((), ())), preferred_element_type=f32)


def block_scores(k, q_block, seg_col, seg_row, start, rows):
    parts = []
    if start:
        s = dot(k[:start], q_block, 1, 1)
        parts.append(jnp.where(seg_col[:start] == seg_row, s, NEG))
    s = dot(k[start : start + rows], q_block, 1, 1)
    row = lax.broadcasted_iota(jnp.int32, s.shape, 0)
    col = lax.broadcasted_iota(jnp.int32, s.shape, 1)
    parts.append(jnp.where((seg_col[start : start + rows] == seg_row) & (row <= col), s, NEG))
    return parts


def attend_kernel(q_ref, k_ref, v_ref, seg_col_ref, seg_row_ref, o_ref, lse_ref, *, rows):
    length = k_ref.shape[0]
    for head in range(2):
        lanes = slice(head * HEAD_DIM, (head + 1) * HEAD_DIM)
        k = k_ref[:, lanes]
        v_t = v_ref[:, lanes].T
        for start in range(0, length, rows):
            stop = start + rows
            parts = block_scores(
                k, q_ref[start:stop, lanes], seg_col_ref, seg_row_ref[:, start:stop], start, rows
            )
            top = jnp.max(parts[-1], axis=0, keepdims=True)
            if start:
                top = jnp.maximum(top, jnp.max(parts[0], axis=0, keepdims=True))
            expo = [jnp.exp(s - top) for s in parts]
            total = sum(jnp.sum(e, axis=0, keepdims=True) for e in expo)
            mixed = dot(v_t[:, start:stop], expo[-1].astype(bf16), 1, 0)
            if start:
                mixed += dot(v_t[:, :start], expo[0].astype(bf16), 1, 0)
            o_ref[start:stop, lanes] = (mixed / total).T.astype(bf16)
            lse_ref[head : head + 1, start:stop] = top + jnp.log(total)


def attend_back_kernel(
    q_ref, k_ref, v_ref, do_ref, lse_ref, seg_col_ref, seg_row_ref, dq_ref, dk_ref, dv_ref, dk_acc, dv_acc, *, rows
):
    length = k_ref.shape[0]
    scale = HEAD_DIM ** (-0.5)
    for head in range(2):
        lanes = slice(head * HEAD_DIM, (head + 1) * HEAD_DIM)
        k = k_ref[:, lanes]
        v = v_ref[:, lanes]
        k_t = k.T
        for start in range(length - rows, -1, -rows):
            stop = start + rows
            q_block = q_ref[start:stop, lanes]
            do_block = do_ref[start:stop, lanes]
            lse = lse_ref[head : head + 1, start:stop]
            parts = block_scores(k, q_block, seg_col_ref, seg_row_ref[:, start:stop], start, rows)
            spans = [(0, start), (start, stop)] if start else [(start, stop)]
            probs = [jnp.exp(s - lse) for s in parts]
            d_probs = [dot(v[lo:hi], do_block, 1, 1) for lo, hi in spans]
            delta = sum(jnp.sum(p * d, axis=0, keepdims=True) for p, d in zip(probs, d_probs))
            dq_t = 0.0
            for (lo, hi), p, d in zip(spans, probs, d_probs):
                ds = (p * (d - delta)).astype(bf16)
                dq_t += dot(k_t[:, lo:hi], ds, 1, 0)
                dk_part = dot(ds, q_block, 1, 0)
                dv_part = dot(p.astype(bf16), do_block, 1, 0)
                if stop == length:
                    dk_acc[lo:hi, :] = dk_part
                    dv_acc[lo:hi, :] = dv_part
                else:
                    dk_acc[lo:hi, :] += dk_part
                    dv_acc[lo:hi, :] += dv_part
            dq_ref[start:stop, lanes] = (dq_t * scale).T.astype(bf16)
        dk_ref[:, lanes] = dk_acc[...].astype(bf16)
        dv_ref[:, lanes] = dv_acc[...].astype(bf16)


def attend(q, k, v, seg_col, seg_row):
    length, width = q.shape
    pairs = width // 128
    wide = pl.BlockSpec((length, 128), lambda p: (0, p))
    return pl.pallas_call(
        lambda *refs: attend_kernel(*refs, rows=min(256, length)),
        out_shape=(
            jax.ShapeDtypeStruct((length, width), bf16),
            jax.ShapeDtypeStruct((pairs, 8, length), f32),
        ),
        grid=(pairs,),
        in_specs=[
            wide,
            wide,
            wide,
            pl.BlockSpec((length, 1), lambda p: (0, 0)),
            pl.BlockSpec((1, length), lambda p: (0, 0)),
        ],
        out_specs=(wide, pl.BlockSpec((None, 8, length), lambda p: (p, 0, 0))),
        compiler_params=pltpu.CompilerParams(vmem_limit_bytes=48 * 1024 * 1024),
        cost_estimate=pl.CostEstimate(
            flops=4 * length * length * width, bytes_accessed=8 * length * width, transcendentals=length * length * 4
        ),
        name="attend",
    )(q, k, v, seg_col, seg_row)


def attend_back(q, k, v, d_mixed, lse, seg_col, seg_row):
    length, width = q.shape
    pairs = width // 128
    wide = pl.BlockSpec((length, 128), lambda p: (0, p))
    return pl.pallas_call(
        lambda *refs: attend_back_kernel(*refs, rows=min(256, length)),
        out_shape=(jax.ShapeDtypeStruct((length, width), bf16),) * 3,
        grid=(pairs,),
        in_specs=[
            wide,
            wide,
            wide,
            wide,
            pl.BlockSpec((None, 8, length), lambda p: (p, 0, 0)),
            pl.BlockSpec((length, 1), lambda p: (0, 0)),
            pl.BlockSpec((1, length), lambda p: (0, 0)),
        ],
        out_specs=(wide, wide, wide),
        scratch_shapes=[pltpu.VMEM((length, HEAD_DIM), f32)] * 2,
        compiler_params=pltpu.CompilerParams(vmem_limit_bytes=48 * 1024 * 1024),
        cost_estimate=pl.CostEstimate(
            flops=10 * length * length * width, bytes_accessed=16 * length * width, transcendentals=length * length * 4
        ),
        name="attend_back",
    )(q, k, v, d_mixed, lse, seg_col, seg_row)


def split_heads(t):
    return t.reshape(t.shape[0], -1, HEAD_DIM).transpose(1, 0, 2)


def join_heads(t):
    return t.transpose(1, 0, 2).reshape(t.shape[1], -1)


def attend_far(q, k, v, allowed):
    def one(item):
        qh, kh, vh = item
        s = jnp.where(allowed, dot(qh, kh, 1, 1), NEG)
        top = jnp.max(s, axis=-1, keepdims=True)
        e = jnp.exp(s - top)
        total = jnp.sum(e, axis=-1, keepdims=True)
        return dot((e / total).astype(bf16), vh, 1, 0), (top + jnp.log(total))[:, 0]

    mixed, lse = lax.map(one, (split_heads(q), split_heads(k), split_heads(v)))
    return join_heads(mixed).astype(bf16), lse


def attend_far_back(q, k, v, d_mixed, lse, allowed):
    def one(item):
        qh, kh, vh, dh, l = item
        p = jnp.exp(jnp.where(allowed, dot(qh, kh, 1, 1), NEG) - l[:, None])
        dp = dot(dh, vh, 1, 1)
        ds = (p * (dp - jnp.sum(p * dp, axis=-1, keepdims=True))).astype(bf16)
        return (
            dot(ds, kh, 1, 0) * HEAD_DIM ** (-0.5),
            dot(ds, qh, 0, 0),
            dot(p.astype(bf16), dh, 0, 0),
        )

    grads = lax.map(one, (split_heads(q), split_heads(k), split_heads(v), split_heads(d_mixed), lse))
    return tuple(join_heads(g) for g in grads)


def standardize(values):
    centered = values - jnp.mean(values, axis=-1, keepdims=True)
    spread = jnp.mean(centered * centered, axis=-1, keepdims=True)
    inverse = lax.rsqrt(spread + 1e-05)
    return centered * inverse, inverse


def norm_backward(grad, xhat, inverse, gain):
    dz = grad * gain
    d_in = inverse * (
        dz - jnp.mean(dz, axis=-1, keepdims=True) - xhat * jnp.mean(dz * xhat, axis=-1, keepdims=True)
    )
    return d_in, jnp.sum(grad * xhat, axis=0), jnp.sum(grad, axis=0)


def build(dp_size, fsdp_size):
    F = fsdp_size
    X = dp_size // 2
    inner = 2 ** ((F.bit_length() - 1) // 2)
    outer = F // inner

    def swap(a):
        return lax.ppermute(a, "dp", [(d, d ^ 1) for d in range(dp_size)])

    def along(a, step_outer, step_inner):
        perm = []
        for o in range(outer):
            for i in range(inner):
                src = ((o + step_outer) % outer) * inner + (i + step_inner) % inner
                perm.append((src, o * inner + i))
        return lax.ppermute(a, "fsdp", perm)

    def gather(a, o, i):
        line = jnp.zeros((outer,) + a.shape, a.dtype)
        for step in range(outer):
            piece = along(a, step, 0) if step else a
            line = lax.dynamic_update_index_in_dim(line, piece, (o + step) % outer, 0)
        if inner == 2:
            other = along(line, 0, 1)
            first = i == 0
            both = jnp.stack([jnp.where(first, line, other), jnp.where(first, other, line)], axis=1)
        else:
            both = jnp.zeros((outer, inner) + a.shape, a.dtype)
            for step in range(inner):
                piece = along(line, 0, step) if step else line
                both = lax.dynamic_update_index_in_dim(both, piece, (i + step) % inner, 1)
        return both.reshape((F,) + a.shape)

    def reduce(a, o, i):
        a = a.reshape((outer, inner) + a.shape[1:])
        total = lax.dynamic_index_in_dim(a, i, 1, keepdims=False).astype(f32)
        for step in range(1, inner):
            total += along(
                lax.dynamic_index_in_dim(a, (i + inner - step) % inner, 1, keepdims=False), 0, step
            ).astype(f32)
        a = total.astype(bf16)
        total = lax.dynamic_index_in_dim(a, o, 0, keepdims=False).astype(f32)
        for step in range(1, outer):
            total += along(
                lax.dynamic_index_in_dim(a, (o + outer - step) % outer, 0, keepdims=False), step, 0
            ).astype(f32)
        a = total.astype(bf16)
        total = a.astype(f32)
        for step in range(1, X):
            total += lax.ppermute(
                a, "dp", [(d, (d + 2 * step) % dp_size) for d in range(dp_size)]
            ).astype(f32)
        return total.astype(bf16)

    def local(
        inputs,
        segments,
        cotangent,
        qkv_weight,
        query_bias,
        value_bias,
        out_weight,
        out_bias,
        norm1_gain,
        norm1_shift,
        up_weight,
        up_bias,
        down_weight,
        down_bias,
        norm2_gain,
        norm2_shift,
    ):
        seqs, block, width = inputs.shape
        hidden = up_weight.shape[1]
        chips = F // (2 * seqs)
        per_core = F // chips // 2
        own = per_core * block
        half = width // 2
        part = width // F
        deep = hidden // F
        core = lax.axis_index("dp") % 2
        f = lax.axis_index("fsdp")
        o, i = f // inner, f % inner
        is_first = core == 0

        def route(k, back):
            perm = []
            for x in range(X):
                for c in range(2):
                    for b in range(F):
                        t = b % per_core
                        to_core = (b // per_core) % 2
                        to_chip = (c * seqs + (t ^ k)) * chips + b // (2 * per_core)
                        pair = ((x * 2 + c) * F + b, (x * 2 + to_core) * F + to_chip)
                        perm.append(pair[::-1] if back else pair)
            return perm

        slot = f % per_core
        seq_here = (f // chips) % seqs

        def to_chips(a):
            got = [
                lax.ppermute(
                    lax.dynamic_index_in_dim(a, slot ^ k, 0, keepdims=False), ("dp", "fsdp"), route(k, False)
                )
                for k in range(seqs)
            ]
            got = jnp.stack(got)
            return jnp.concatenate(
                [lax.dynamic_index_in_dim(got, t ^ seq_here, 0) for t in range(per_core)], axis=0
            )

        def to_blocks(a):
            a = a.reshape(per_core, block, width)
            got = [
                lax.ppermute(
                    lax.dynamic_index_in_dim(a, seq_here ^ k, 0, keepdims=False), ("dp", "fsdp"), route(k, True)
                )
                for k in range(seqs)
            ]
            got = jnp.stack(got)
            return jnp.concatenate(
                [lax.dynamic_index_in_dim(got, s ^ slot, 0) for s in range(seqs)], axis=0
            )

        def in_order(mine, other, axis):
            return jnp.concatenate(
                [jnp.where(is_first, mine, other), jnp.where(is_first, other, mine)], axis=axis
            )

        small = jnp.concatenate(
            [query_bias, value_bias, out_bias, norm1_gain, norm1_shift, down_bias, norm2_gain, norm2_shift, up_bias]
        )
        heads_w = jnp.concatenate(
            [lax.dynamic_slice_in_dim(qkv_weight, n * width + core * half, half, 1) for n in range(3)], axis=1
        )
        lanes = heads_w.shape[1]
        first_pack = jnp.concatenate(
            [heads_w, jnp.pad(small[None], ((0, 7), (0, lanes - small.shape[0])))], axis=0
        )
        first_all = gather(first_pack, o, i)
        w_heads = first_all[:, :part].reshape(width, lanes)
        small_all = first_all[:, part].astype(f32)
        vectors = small_all[:, : 8 * part].reshape(F, 8, part).transpose(1, 0, 2).reshape(8, width)
        b_query, b_value, b_out, gain1, shift1, b_down, gain2, shift2 = [vectors[n] for n in range(8)]
        b_up_all = small_all[:, 8 * part : 8 * part + deep].reshape(F, 2, deep // 2)

        seg_row_own = jnp.pad(segments.astype(bf16)[:, None, :], ((0, 0), (0, 7), (0, width - block)))
        tokens = to_chips(jnp.concatenate([inputs, seg_row_own], axis=1))
        tokens_other = swap(tokens)
        grad_low = to_chips(cotangent).reshape(own, width)

        up_half = lax.dynamic_index_in_dim(
            up_weight.reshape(part, F, 2, deep // 2), core, 2, keepdims=False
        ).reshape(part, hidden // 2)
        out_half = lax.dynamic_slice_in_dim(out_weight, core * half, half, 1)
        down_half = lax.dynamic_slice_in_dim(down_weight, core * (deep // 2), deep // 2, 0)
        second_all = gather(jnp.concatenate([up_half, out_half], axis=1), o, i).reshape(width, -1)
        second_other = swap(second_all)
        third_all = gather(down_half, o, i).reshape(hidden // 2, width)
        third_other = swap(third_all)
        ups = (second_all[:, : hidden // 2], second_other[:, : hidden // 2])
        downs = (third_all, third_other)
        w_out = in_order(second_all[:, hidden // 2 :], second_other[:, hidden // 2 :], 1)

        x_own = tokens[:, :block].reshape(own, width).astype(f32)
        x_all = in_order(
            tokens[:, :block].reshape(own, width), tokens_other[:, :block].reshape(own, width), 0
        ).astype(f32)
        xhat_all, _ = standardize(x_all)
        hidden1 = (xhat_all * gain1 + shift1).astype(bf16)
        seg = in_order(
            tokens[:, block, :block].reshape(own), tokens_other[:, block, :block].reshape(own), 0
        ).astype(f32)
        joined = jnp.dot(hidden1, w_heads, preferred_element_type=f32)
        bq = lax.dynamic_slice_in_dim(b_query, core * half, half)
        bv = lax.dynamic_slice_in_dim(b_value, core * half, half)
        q = (joined[:, :half] + bq).astype(bf16) * bf16(HEAD_DIM ** (-0.5))
        k = joined[:, half : 2 * half].astype(bf16)
        v = (joined[:, 2 * half :] + bv).astype(bf16)
        if chips == 1:
            seg_col, seg_row = seg[:, None], seg[None, :]
            mixed, lse = attend(q, k, v, seg_col, seg_row)
        else:
            groups = [[g * chips + n for n in range(chips)] for g in range(F // chips)]
            k, v, seg_keys = (
                lax.all_gather(t, "fsdp", axis=0, tiled=True, axis_index_groups=groups) for t in (k, v, seg)
            )
            position = (f % chips) * 2 * own + jnp.arange(2 * own, dtype=jnp.int32)
            allowed = (jnp.arange(k.shape[0], dtype=jnp.int32)[None, :] <= position[:, None]) & (
                seg_keys[None, :] == seg[:, None]
            )
            mixed, lse = attend_far(q, k, v, allowed)

        mixed_other = swap(lax.dynamic_slice_in_dim(mixed, (1 - core) * own, own, 0))
        mixed_own = in_order(lax.dynamic_slice_in_dim(mixed, core * own, own, 0), mixed_other, 1)
        midway = x_own + jnp.dot(mixed_own, w_out, preferred_element_type=f32) + b_out
        xhat2, inverse2 = standardize(midway)
        hidden2 = (xhat2 * gain2 + shift2).astype(bf16)
        pre_acts, activs, pulls = [], [], []
        result = midway + b_down
        for n in range(2):
            b_up = lax.dynamic_index_in_dim(b_up_all, core ^ n, 1, keepdims=False).reshape(hidden // 2)
            pre = jnp.dot(hidden2, ups[n], preferred_element_type=f32) + b_up
            act, pull = jax.vjp(lambda t: jax.nn.gelu(t, approximate=True), pre)
            act = act.astype(bf16)
            activs.append(act)
            pulls.append(pull)
            result += jnp.dot(act, downs[n], preferred_element_type=f32)
        output = to_blocks(result.astype(bf16))

        grad_out = grad_low.astype(f32)
        d_down_b = jnp.sum(grad_out, axis=0)
        d_pres = [None, None]
        d_downs = [None, None]
        d_ups = [None, None]
        for n in (1, 0):
            d_downs[n] = dot(activs[n], grad_low, 0, 0).astype(bf16)
            d_pres[n] = pulls[n](dot(grad_low, downs[n], 1, 1))[0].astype(bf16)
            d_ups[n] = dot(hidden2, d_pres[n], 0, 0).astype(bf16)
        d_down_sum = (d_downs[0].astype(f32) + swap(d_downs[1]).astype(f32)).astype(bf16)
        d_down_red = reduce(d_down_sum.reshape(F, deep // 2, width), o, i)
        d_hidden2 = dot(d_pres[0], ups[0], 1, 1) + dot(d_pres[1], ups[1], 1, 1)
        d_up_bs = [jnp.sum(t.astype(f32), axis=0) for t in d_pres]
        d_norm2, d_gain2, d_shift2 = norm_backward(d_hidden2, xhat2, inverse2, gain2)
        d_mid = grad_out + d_norm2
        d_branch = d_mid.astype(bf16)
        d_mixed = dot(d_branch, w_out, 1, 1).astype(bf16)
        d_mixed_other = swap(lax.dynamic_slice_in_dim(d_mixed, (1 - core) * half, half, 1))
        d_out = dot(mixed_own, d_branch, 0, 0).astype(bf16)
        d_out_b = jnp.sum(d_branch.astype(f32), axis=0)
        give = jnp.concatenate([d_ups[1], lax.dynamic_slice_in_dim(d_out, (1 - core) * half, half, 1)], axis=1)
        keep = jnp.concatenate([d_ups[0], lax.dynamic_slice_in_dim(d_out, core * half, half, 1)], axis=1)
        d_second = (keep.astype(f32) + swap(give).astype(f32)).astype(bf16)
        d_second_red = reduce(d_second.reshape(F, part, -1), o, i)

        d_heads = in_order(lax.dynamic_slice_in_dim(d_mixed, core * half, half, 1), d_mixed_other, 0)
        if chips == 1:
            dq, dk, dv = attend_back(q, k, v, d_heads, lse, seg_col, seg_row)
        else:
            dq, dk, dv = attend_far_back(q, k, v, d_heads, lse, allowed)
            dk, dv = (
                lax.psum_scatter(
                    t.astype(bf16), "fsdp", scatter_dimension=0, tiled=True, axis_index_groups=groups
                )
                for t in (dk, dv)
            )
            dq = dq.astype(bf16)
        d_joined = jnp.concatenate([dq, dk, dv], axis=1)
        d_hidden1 = dot(d_joined, w_heads, 1, 1)
        d_hidden1_other = swap(lax.dynamic_slice_in_dim(d_hidden1, (1 - core) * own, own, 0).astype(bf16))
        d_hidden1 = lax.dynamic_slice_in_dim(d_hidden1, core * own, own, 0) + d_hidden1_other.astype(f32)
        xhat1, inverse1 = standardize(x_own)
        d_norm1, d_gain1, d_shift1 = norm_backward(d_hidden1, xhat1, inverse1, gain1)
        d_inputs = to_blocks((d_mid + d_norm1).astype(bf16))

        d_w_heads = dot(hidden1, d_joined, 0, 0)
        d_bias = jnp.sum(d_joined.astype(f32), axis=0)

        def placed(vector):
            return lax.dynamic_update_slice_in_dim(jnp.zeros((width,), f32), vector, core * half, 0)

        d_vectors = jnp.stack(
            [placed(d_bias[:half]), placed(d_bias[2 * half :]), d_out_b, d_gain1, d_shift1, d_down_b, d_gain2, d_shift2]
        )
        d_vectors = d_vectors.reshape(8, F, part).transpose(1, 0, 2).reshape(F, 8 * part)
        d_up_b = in_order(d_up_bs[0].reshape(F, 1, deep // 2), d_up_bs[1].reshape(F, 1, deep // 2), 1)
        d_small = jnp.concatenate([d_vectors, d_up_b.reshape(F, deep)], axis=1)
        d_small = jnp.pad(d_small[:, None], ((0, 0), (0, 7), (0, lanes - d_small.shape[1])))
        d_first = jnp.concatenate([d_w_heads.reshape(F, part, lanes), d_small], axis=1).astype(bf16)
        d_first_red = reduce(d_first, o, i)

        first_o = swap(d_first_red)
        second_o = swap(d_second_red)
        down_o = swap(d_down_red)
        cols = half
        pieces = []
        for n in range(3):
            sl = slice(n * cols, (n + 1) * cols)
            pieces.append(in_order(d_first_red[:part, sl], first_o[:part, sl], 1))
        d_qkv_w = jnp.concatenate(pieces, axis=1).astype(f32)
        small_sum = d_first_red[part].astype(f32) + first_o[part].astype(f32)
        vec = [small_sum[n * part : (n + 1) * part] for n in range(8)]
        d_up_b = small_sum[8 * part : 8 * part + deep]
        up_m = d_second_red[:, : hidden // 2].reshape(part, F, 1, deep // 2)
        up_o = second_o[:, : hidden // 2].reshape(part, F, 1, deep // 2)
        d_up_w = in_order(up_m, up_o, 2).reshape(part, hidden).astype(f32)
        d_out_w = in_order(d_second_red[:, hidden // 2 :], second_o[:, hidden // 2 :], 1).astype(f32)
        d_down_w = in_order(d_down_red, down_o, 0).astype(f32)
        return (
            output,
            d_inputs,
            d_qkv_w,
            vec[0],
            vec[1],
            d_out_w,
            vec[2],
            vec[3],
            vec[4],
            d_up_w,
            d_up_b,
            d_down_w,
            vec[5],
            vec[6],
            vec[7],
        )

    return local


def solution(mesh):
    in_specs = (
        P("dp", "fsdp", None),
        P("dp", "fsdp"),
        P("dp", "fsdp", None),
        P("fsdp", None),
        P("fsdp"),
        P("fsdp"),
        P("fsdp", None),
        P("fsdp"),
        P("fsdp"),
        P("fsdp"),
        P("fsdp", None),
        P("fsdp"),
        P("fsdp", None),
        P("fsdp"),
        P("fsdp"),
        P("fsdp"),
    )
    out_specs = (
        P("dp", "fsdp", None),
        P("dp", "fsdp", None),
        P("fsdp", None),
        P("fsdp"),
        P("fsdp"),
        P("fsdp", None),
        P("fsdp"),
        P("fsdp"),
        P("fsdp"),
        P("fsdp", None),
        P("fsdp"),
        P("fsdp", None),
        P("fsdp"),
        P("fsdp"),
        P("fsdp"),
    )
    local = build(mesh.shape["dp"], mesh.shape["fsdp"])
    return jax.shard_map(local, mesh=mesh, in_specs=in_specs, out_specs=out_specs, check_vma=False)
```

```python
import jax
import jax.numpy as jnp
from jax import lax
from jax.experimental import pallas as pl
from jax.experimental.pallas import tpu as pltpu
from jax.sharding import PartitionSpec as P

HEAD_DIM = 64
NEG = -1e30
GELU_A = 0.7978845608
GELU_B = 0.044715
f32 = jnp.float32
bf16 = jnp.bfloat16


def dot(a, b, ca, cb):
    return lax.dot_general(a, b, (((ca,), (cb,)), ((), ())), preferred_element_type=f32)


def block_scores(k, q_block, seg_col, seg_row, start, rows):
    parts = []
    if start:
        s = dot(k[:start], q_block, 1, 1)
        parts.append(jnp.where(seg_col[:start] == seg_row, s, NEG))
    s = dot(k[start : start + rows], q_block, 1, 1)
    row = lax.broadcasted_iota(jnp.int32, s.shape, 0)
    col = lax.broadcasted_iota(jnp.int32, s.shape, 1)
    parts.append(jnp.where((seg_col[start : start + rows] == seg_row) & (row <= col), s, NEG))
    return parts


def attend_kernel(q_ref, k_ref, v_ref, seg_col_ref, seg_row_ref, o_ref, lse_ref, *, rows):
    length = k_ref.shape[0]
    for head in range(2):
        lanes = slice(head * HEAD_DIM, (head + 1) * HEAD_DIM)
        k = k_ref[:, lanes]
        v_t = v_ref[:, lanes].T
        for start in range(0, length, rows):
            stop = start + rows
            parts = block_scores(
                k, q_ref[start:stop, lanes], seg_col_ref, seg_row_ref[:, start:stop], start, rows
            )
            top = jnp.max(parts[-1], axis=0, keepdims=True)
            if start:
                top = jnp.maximum(top, jnp.max(parts[0], axis=0, keepdims=True))
            expo = [jnp.exp(s - top) for s in parts]
            total = sum(jnp.sum(e, axis=0, keepdims=True) for e in expo)
            mixed = dot(v_t[:, start:stop], expo[-1].astype(bf16), 1, 0)
            if start:
                mixed += dot(v_t[:, :start], expo[0].astype(bf16), 1, 0)
            o_ref[start:stop, lanes] = (mixed / total).T.astype(bf16)
            lse_ref[head : head + 1, start:stop] = top + jnp.log(total)


def attend_back_kernel(
    q_ref, k_ref, v_ref, do_ref, lse_ref, seg_col_ref, seg_row_ref, dq_ref, dk_ref, dv_ref, dk_acc, dv_acc, *, rows
):
    length = k_ref.shape[0]
    scale = HEAD_DIM ** (-0.5)
    for head in range(2):
        lanes = slice(head * HEAD_DIM, (head + 1) * HEAD_DIM)
        k = k_ref[:, lanes]
        v = v_ref[:, lanes]
        k_t = k.T
        for start in range(length - rows, -1, -rows):
            stop = start + rows
            q_block = q_ref[start:stop, lanes]
            do_block = do_ref[start:stop, lanes]
            lse = lse_ref[head : head + 1, start:stop]
            parts = block_scores(k, q_block, seg_col_ref, seg_row_ref[:, start:stop], start, rows)
            spans = [(0, start), (start, stop)] if start else [(start, stop)]
            probs = [jnp.exp(s - lse) for s in parts]
            d_probs = [dot(v[lo:hi], do_block, 1, 1) for lo, hi in spans]
            delta = sum(jnp.sum(p * d, axis=0, keepdims=True) for p, d in zip(probs, d_probs))
            dq_t = 0.0
            for (lo, hi), p, d in zip(spans, probs, d_probs):
                ds = (p * (d - delta)).astype(bf16)
                dq_t += dot(k_t[:, lo:hi], ds, 1, 0)
                dk_part = dot(ds, q_block, 1, 0)
                dv_part = dot(p.astype(bf16), do_block, 1, 0)
                if stop == length:
                    dk_acc[lo:hi, :] = dk_part
                    dv_acc[lo:hi, :] = dv_part
                else:
                    dk_acc[lo:hi, :] += dk_part
                    dv_acc[lo:hi, :] += dv_part
            dq_ref[start:stop, lanes] = (dq_t * scale).T.astype(bf16)
        dk_ref[:, lanes] = dk_acc[...].astype(bf16)
        dv_ref[:, lanes] = dv_acc[...].astype(bf16)


def attend(q, k, v, seg_col, seg_row):
    length, width = q.shape
    pairs = width // 128
    wide = pl.BlockSpec((length, 128), lambda p: (0, p))
    return pl.pallas_call(
        lambda *refs: attend_kernel(*refs, rows=min(256, length)),
        out_shape=(
            jax.ShapeDtypeStruct((length, width), bf16),
            jax.ShapeDtypeStruct((pairs, 8, length), f32),
        ),
        grid=(pairs,),
        in_specs=[
            wide,
            wide,
            wide,
            pl.BlockSpec((length, 1), lambda p: (0, 0)),
            pl.BlockSpec((1, length), lambda p: (0, 0)),
        ],
        out_specs=(wide, pl.BlockSpec((None, 8, length), lambda p: (p, 0, 0))),
        compiler_params=pltpu.CompilerParams(vmem_limit_bytes=48 * 1024 * 1024),
        cost_estimate=pl.CostEstimate(
            flops=28 * length * length * width, bytes_accessed=8 * length * width, transcendentals=length * length * 4
        ),
        name="attend",
    )(q, k, v, seg_col, seg_row)


def attend_back(q, k, v, d_mixed, lse, seg_col, seg_row):
    length, width = q.shape
    pairs = width // 128
    wide = pl.BlockSpec((length, 128), lambda p: (0, p))
    return pl.pallas_call(
        lambda *refs: attend_back_kernel(*refs, rows=min(256, length)),
        out_shape=(jax.ShapeDtypeStruct((length, width), bf16),) * 3,
        grid=(pairs,),
        in_specs=[
            wide,
            wide,
            wide,
            wide,
            pl.BlockSpec((None, 8, length), lambda p: (p, 0, 0)),
            pl.BlockSpec((length, 1), lambda p: (0, 0)),
            pl.BlockSpec((1, length), lambda p: (0, 0)),
        ],
        out_specs=(wide, wide, wide),
        scratch_shapes=[pltpu.VMEM((length, HEAD_DIM), f32)] * 2,
        compiler_params=pltpu.CompilerParams(vmem_limit_bytes=48 * 1024 * 1024),
        cost_estimate=pl.CostEstimate(
            flops=50 * length * length * width, bytes_accessed=16 * length * width, transcendentals=length * length * 4
        ),
        name="attend_back",
    )(q, k, v, d_mixed, lse, seg_col, seg_row)


def split_heads(t):
    return t.reshape(t.shape[0], -1, HEAD_DIM).transpose(1, 0, 2)


def join_heads(t):
    return t.transpose(1, 0, 2).reshape(t.shape[1], -1)


def attend_far(q, k, v, allowed):
    def one(item):
        qh, kh, vh = item
        s = jnp.where(allowed, dot(qh, kh, 1, 1), NEG)
        top = jnp.max(s, axis=-1, keepdims=True)
        e = jnp.exp(s - top)
        total = jnp.sum(e, axis=-1, keepdims=True)
        return dot((e / total).astype(bf16), vh, 1, 0), (top + jnp.log(total))[:, 0]

    mixed, lse = lax.map(one, (split_heads(q), split_heads(k), split_heads(v)))
    return join_heads(mixed).astype(bf16), lse


def attend_far_back(q, k, v, d_mixed, lse, allowed):
    def one(item):
        qh, kh, vh, dh, l = item
        p = jnp.exp(jnp.where(allowed, dot(qh, kh, 1, 1), NEG) - l[:, None])
        dp = dot(dh, vh, 1, 1)
        ds = (p * (dp - jnp.sum(p * dp, axis=-1, keepdims=True))).astype(bf16)
        return (
            dot(ds, kh, 1, 0) * HEAD_DIM ** (-0.5),
            dot(ds, qh, 0, 0),
            dot(p.astype(bf16), dh, 0, 0),
        )

    grads = lax.map(one, (split_heads(q), split_heads(k), split_heads(v), split_heads(d_mixed), lse))
    return tuple(join_heads(g) for g in grads)


def place(pieces, indices, shape, spans):
    table = jnp.stack([jnp.asarray(v, jnp.int32) for index in indices for v in index])
    offsets = []
    for index in indices:
        offsets.append(sum(len(t) for t in indices[: len(offsets)]))

    def kernel(table_ref, *refs):
        out_ref, sems = refs[len(pieces)], refs[len(pieces) + 1]
        copies = []
        for n, span in enumerate(spans):
            spot = tuple(table_ref[offsets[n] + m] for m in range(len(indices[n])))
            target = out_ref.at[spot] if span is None else out_ref.at[(span,) + spot]
            copies.append(pltpu.make_async_copy(refs[n], target, sems.at[n]))
        for copy in copies:
            copy.start()
        for copy in copies:
            copy.wait()

    size = 2
    for extent in shape:
        size *= extent
    return pl.pallas_call(
        kernel,
        out_shape=jax.ShapeDtypeStruct(shape, pieces[0].dtype),
        in_specs=[pl.BlockSpec(memory_space=pltpu.SMEM)] + [pl.BlockSpec(memory_space=pl.ANY)] * len(pieces),
        out_specs=pl.BlockSpec(memory_space=pltpu.VMEM),
        scratch_shapes=[pltpu.SemaphoreType.DMA((len(pieces),))],
        compiler_params=pltpu.CompilerParams(vmem_limit_bytes=2 * size + (8 << 20)),
        cost_estimate=pl.CostEstimate(flops=0, bytes_accessed=2 * size, transcendentals=0),
        name="place",
    )(table, *pieces)


def after(a, *others):
    return lax.optimization_barrier((a,) + others)[0] if others else a


def row_pieces(deep):
    pieces = []
    for half in range(2):
        at, stop = half * (deep // 2), (half + 1) * (deep // 2)
        while at < stop:
            end = min(stop, (at // 128 + 1) * 128)
            pieces.append((half, at - half * (deep // 2), at // 128, at % 128, at % 128 + end - at))
            at = end
    return pieces


def unpack_small(small, part, deep):
    count = small.shape[0]

    def kernel(in_ref, vec_ref, up_ref):
        for f in range(count):
            rows = in_ref[f].astype(f32)
            vec_ref[:, f * part : (f + 1) * part] = rows[:8, :part]
            for half, at, row, lo, hi in row_pieces(deep):
                start = f * (deep // 2) + at
                up_ref[half : half + 1, start : start + hi - lo] = rows[8 + row : 9 + row, lo:hi]

    return pl.pallas_call(
        kernel,
        out_shape=(
            jax.ShapeDtypeStruct((8, count * part), f32),
            jax.ShapeDtypeStruct((2, count * (deep // 2)), f32),
        ),
        name="unpack_small",
    )(small)


def pack_small(core, rows_in, d_bias, d_up_mine, d_up_other, count, total_rows):
    width = rows_in[0].shape[1]
    part, half = width // count, width // 2
    deep = 2 * d_up_mine.shape[1] // count
    core = jnp.reshape(core, (1,)).astype(jnp.int32)

    def kernel(core_ref, bias_ref, up_m_ref, up_o_ref, *refs):
        out_ref, vec, up = refs[-3], refs[-2], refs[-1]
        first = core_ref[0] == 0
        none = jnp.zeros((1, half), f32)
        for n, lo in enumerate((0, 2 * half)):
            mine = bias_ref[:, lo : lo + half]
            vec[n : n + 1, :half] = jnp.where(first, mine, none)
            vec[n : n + 1, half:] = jnp.where(first, none, mine)
        for n in range(6):
            vec[2 + n : 3 + n, :] = refs[n][...]
        up[0:1, :] = jnp.where(first, up_m_ref[...], up_o_ref[...])
        up[1:2, :] = jnp.where(first, up_o_ref[...], up_m_ref[...])
        out_ref[...] = jnp.zeros_like(out_ref)
        for f in range(count):
            out_ref[f, 0:8, :part] = vec[:, f * part : (f + 1) * part]
            for which, at, row, lo, hi in row_pieces(deep):
                start = f * (deep // 2) + at
                out_ref[f, 8 + row : 9 + row, lo:hi] = up[which : which + 1, start : start + hi - lo]

    return pl.pallas_call(
        kernel,
        out_shape=jax.ShapeDtypeStruct((count, total_rows, 128), f32),
        in_specs=[pl.BlockSpec(memory_space=pltpu.SMEM)] + [pl.BlockSpec(memory_space=pltpu.VMEM)] * 9,
        scratch_shapes=[pltpu.VMEM((8, width), f32), pltpu.VMEM((2, d_up_mine.shape[1]), f32)],
        name="pack_small",
    )(core, d_bias, d_up_mine, d_up_other, *rows_in)


def weave(core, mine, other, count):
    rows, cols = mine.shape
    step = cols // count
    core = jnp.reshape(core, (1,)).astype(jnp.int32)

    def kernel(core_ref, mine_ref, other_ref, out_ref):
        first = core_ref[0] == 0
        a, b = mine_ref[...].astype(f32), other_ref[...].astype(f32)
        low, high = jnp.where(first, a, b), jnp.where(first, b, a)
        for n in range(count):
            out_ref[:, 2 * n * step : (2 * n + 1) * step] = low[:, n * step : (n + 1) * step]
            out_ref[:, (2 * n + 1) * step : (2 * n + 2) * step] = high[:, n * step : (n + 1) * step]

    return pl.pallas_call(
        kernel,
        out_shape=jax.ShapeDtypeStruct((rows, 2 * cols), f32),
        in_specs=[pl.BlockSpec(memory_space=pltpu.SMEM)] + [pl.BlockSpec(memory_space=pltpu.VMEM)] * 2,
        name="weave",
    )(core, mine, other)


def standardize(values):
    centered = values - jnp.mean(values, axis=-1, keepdims=True)
    spread = jnp.mean(centered * centered, axis=-1, keepdims=True)
    inverse = lax.rsqrt(spread + 1e-05)
    return centered * inverse, inverse


def norm_backward(grad, xhat, inverse, gain):
    dz = grad * gain
    d_in = inverse * (
        dz - jnp.mean(dz, axis=-1, keepdims=True) - xhat * jnp.mean(dz * xhat, axis=-1, keepdims=True)
    )
    return d_in, jnp.sum(grad * xhat, axis=0, keepdims=True), jnp.sum(grad, axis=0, keepdims=True)


def build(dp_size, fsdp_size):
    F = fsdp_size
    X = dp_size // 2
    inner = 2 ** ((F.bit_length() - 1) // 2)
    outer = F // inner

    def swap(a):
        return lax.ppermute(a, "dp", [(d, d ^ 1) for d in range(dp_size)])

    def along(a, step_outer, step_inner):
        perm = []
        for o in range(outer):
            for i in range(inner):
                src = ((o + step_outer) % outer) * inner + (i + step_inner) % inner
                perm.append((src, o * inner + i))
        return lax.ppermute(a, "fsdp", perm)

    def across(a, step):
        return lax.ppermute(a, "dp", [((d + 2 * step) % dp_size, d) for d in range(dp_size)])

    def gather_line(a, o, *late):
        pieces = [after(a, *late)] + [along(a, step, 0) for step in range(1, outer)]
        return place(
            pieces, [((o + step) % outer,) for step in range(outer)], (outer,) + a.shape, [None] * outer
        )

    cube = inner == 2 and X == 2 and outer % 2 == 0
    cut = outer // 2

    def gather_sides(line):
        return (across(line, 1), along(line, 0, 1)) if cube else ()

    def gather_rest(line, sides, i, x):
        shape = (outer, inner, X) + line.shape[1:]
        if cube:
            by_x, by_y = sides
            low, high = across(by_y[:cut], 1), along(by_x[cut:], 0, 1)
            return place(
                [line, by_x, by_y, low, high],
                [(i, x), (i, 1 - x), (1 - i, x), (1 - i, 1 - x), (1 - i, 1 - x)],
                shape,
                [slice(None)] * 3 + [slice(0, cut), slice(cut, outer)],
            )
        plane = jnp.zeros((outer, X) + line.shape[1:], line.dtype)
        for step in range(X):
            plane = lax.dynamic_update_index_in_dim(plane, across(line, step) if step else line, (x + step) % X, 1)
        both = jnp.zeros(shape, line.dtype)
        for step in range(inner):
            both = lax.dynamic_update_index_in_dim(both, along(plane, 0, step) if step else plane, (i + step) % inner, 1)
        return both

    def pick(a, index, axis):
        return lax.dynamic_index_in_dim(a, index, axis, keepdims=False)

    def part(a, di, dx, i, x):
        return pick(pick(a, i ^ di, 1), x ^ dx, 1)

    def reduce_far(a, i, x):
        if not cube:
            return a, ()
        far = part(a, 1, 1, i, x)
        low, high = lax.optimization_barrier((far[:cut], far[cut:]))
        return a, (along(low, 0, 1), across(high, 1))

    def reduce_sides(state, i, x, late_far, late_sides):
        a, far = state
        if cube:
            here = after(a, *late_far)
            to_x, to_y = part(here, 0, 1, i, x), part(here, 1, 0, i, x)
            from_y, from_x = far
            to_x = jnp.concatenate([(to_x[:cut].astype(f32) + from_y.astype(f32)).astype(bf16), to_x[cut:]])
            to_y = jnp.concatenate([to_y[:cut], (to_y[cut:].astype(f32) + from_x.astype(f32)).astype(bf16)])
            to_x, to_y = lax.optimization_barrier((to_x, to_y))
            own = part(after(a, *late_sides), 0, 0, i, x)
            return (own.astype(f32) + across(to_x, 1).astype(f32) + along(to_y, 0, 1).astype(f32)).astype(bf16)
        total = pick(a, x, 2).astype(f32)
        for step in range(1, X):
            total += across(pick(a, (x + X - step) % X, 2), step).astype(f32)
        a = total.astype(bf16)
        total = pick(a, i, 1).astype(f32)
        for step in range(1, inner):
            total += along(pick(a, (i + inner - step) % inner, 1), 0, step).astype(f32)
        return total.astype(bf16)

    def reduce_line(a, o, *late):
        terms = lax.optimization_barrier(tuple(pick(a, (o + outer - step) % outer, 0) for step in range(1, outer)))
        total = pick(after(a, *late), o, 0).astype(f32)
        for step in range(1, outer):
            total += along(terms[step - 1], step, 0).astype(f32)
        return total.astype(bf16)

    def gather_x(a, x):
        if X == 2:
            other = across(a, 1)
            return jnp.concatenate([jnp.where(x == 0, a, other), jnp.where(x == 0, other, a)], axis=0)
        full = jnp.zeros((X,) + a.shape, a.dtype)
        for step in range(X):
            full = lax.dynamic_update_index_in_dim(full, across(a, step) if step else a, (x + step) % X, 0)
        return full.reshape((X * a.shape[0],) + a.shape[1:])

    def local(
        inputs,
        segments,
        cotangent,
        qkv_weight,
        query_bias,
        value_bias,
        out_weight,
        out_bias,
        norm1_gain,
        norm1_shift,
        up_weight,
        up_bias,
        down_weight,
        down_bias,
        norm2_gain,
        norm2_shift,
    ):
        seqs, block, width = inputs.shape
        hidden = up_weight.shape[1]
        chips = F // (2 * seqs)
        per_core = F // chips // 2
        own = per_core * block
        half = width // 2
        part = width // F
        deep = hidden // F
        core = lax.axis_index("dp") % 2
        x = lax.axis_index("dp") // 2
        f = lax.axis_index("fsdp")
        o, i = f // inner, f % inner
        is_first = core == 0

        def route(k, back):
            perm = []
            for plane in range(X):
                for c in range(2):
                    for b in range(F):
                        t = b % per_core
                        to_core = (b // per_core) % 2
                        to_chip = (c * seqs + (t ^ k)) * chips + b // (2 * per_core)
                        pair = ((plane * 2 + c) * F + b, (plane * 2 + to_core) * F + to_chip)
                        perm.append(pair[::-1] if back else pair)
            return perm

        slot = f % per_core
        seq_here = (f // chips) % seqs

        def to_chips(a):
            got = [
                lax.ppermute(
                    lax.dynamic_index_in_dim(a, slot ^ k, 0, keepdims=False), ("dp", "fsdp"), route(k, False)
                )
                for k in range(seqs)
            ]
            got = jnp.stack(got)
            return jnp.concatenate(
                [lax.dynamic_index_in_dim(got, t ^ seq_here, 0) for t in range(per_core)], axis=0
            )

        def to_blocks(a, *late):
            a = a.reshape(per_core, block, width)
            got = [
                lax.ppermute(
                    lax.dynamic_index_in_dim(a, seq_here ^ k, 0, keepdims=False), ("dp", "fsdp"), route(k, True)
                )
                for k in range(seqs)
            ]
            got[0] = after(got[0], *late)
            got = jnp.stack(got)
            return jnp.concatenate(
                [lax.dynamic_index_in_dim(got, s ^ slot, 0) for s in range(seqs)], axis=0
            )

        def in_order(mine, other, axis):
            return jnp.concatenate(
                [jnp.where(is_first, mine, other), jnp.where(is_first, other, mine)], axis=axis
            )

        heads_w = jnp.concatenate(
            [lax.dynamic_slice_in_dim(qkv_weight, n * width + core * half, half, 1) for n in range(3)], axis=1
        )
        lanes = heads_w.shape[1]

        def x_rows(a):
            rows = a.shape[0] // X
            return lax.dynamic_slice_in_dim(a, x * rows, rows, 0)

        slim = part // X
        deep_rows = -(-deep // 128)
        wide = -(-(8 + deep_rows) // slim)
        singles = (query_bias, value_bias, out_bias, norm1_gain, norm1_shift, down_bias, norm2_gain, norm2_shift)
        row = lax.broadcasted_iota(jnp.int32, (slim * wide, 128), 0)
        small = jnp.pad(
            jnp.pad(up_bias, (0, deep_rows * 128 - deep)).reshape(deep_rows, 128),
            ((8, slim * wide - 8 - deep_rows), (0, 0)),
        )
        for n, vector in enumerate(singles):
            small = jnp.where(row == n, jnp.pad(vector, (0, 128 - part))[None, :], small)
        first_line = gather_line(
            jnp.concatenate([x_rows(heads_w), small.reshape(slim, wide * 128)], axis=1), o
        )
        first_sides = gather_sides(first_line)

        seg_row_own = jnp.pad(segments.astype(bf16)[:, None, :], ((0, 0), (0, 7), (0, width - block)))
        tokens = to_chips(jnp.concatenate([inputs, seg_row_own], axis=1))
        tokens_other = swap(tokens)

        first_all = gather_rest(first_line, first_sides, i, x)
        w_heads = first_all.reshape(width, lanes + wide * 128)[:, :lanes]
        small_all = first_all[:, :, 0, :, lanes:].reshape(F, slim * wide, 128)
        vectors, b_up_all = unpack_small(small_all, part, deep)
        b_query, b_value, b_out, gain1, shift1, b_down, gain2, shift2 = [vectors[n : n + 1] for n in range(8)]

        up_half = pick(x_rows(up_weight).reshape(slim, F, 2, deep // 2), core, 2).reshape(slim, hidden // 2)
        out_half = lax.dynamic_slice_in_dim(x_rows(out_weight), core * half, half, 1)
        down_half = x_rows(lax.dynamic_slice_in_dim(down_weight, core * (deep // 2), deep // 2, 0))
        second_pack = after(
            jnp.concatenate([up_half, out_half], axis=1), tokens_other, first_line, *first_sides
        )

        x_own = tokens[:, :block].reshape(own, width).astype(f32)
        x_all = in_order(
            tokens[:, :block].reshape(own, width), tokens_other[:, :block].reshape(own, width), 0
        ).astype(f32)
        xhat_all, _ = standardize(x_all)
        hidden1 = (xhat_all * gain1 + shift1).astype(bf16)
        seg = in_order(
            tokens[:, block, :block].reshape(own), tokens_other[:, block, :block].reshape(own), 0
        ).astype(f32)
        joined = jnp.dot(hidden1, w_heads, preferred_element_type=f32)
        bq = jnp.where(is_first, b_query[:, :half], b_query[:, half:])
        bv = jnp.where(is_first, b_value[:, :half], b_value[:, half:])
        q = (joined[:, :half] + bq).astype(bf16) * bf16(HEAD_DIM ** (-0.5))
        k = joined[:, half : 2 * half].astype(bf16)
        v = (joined[:, 2 * half :] + bv).astype(bf16)
        second_line = gather_line(second_pack, o, q)
        second_sides = gather_sides(second_line)
        third_pack = after(down_half, second_line)
        q = after(q, second_line)
        if chips == 1:
            seg_col, seg_row = seg[:, None], seg[None, :]
            mixed, lse = attend(q, k, v, seg_col, seg_row)
        else:
            groups = [[g * chips + n for n in range(chips)] for g in range(F // chips)]
            k, v, seg_keys = (
                lax.all_gather(t, "fsdp", axis=0, tiled=True, axis_index_groups=groups) for t in (k, v, seg)
            )
            position = (f % chips) * 2 * own + jnp.arange(2 * own, dtype=jnp.int32)
            allowed = (jnp.arange(k.shape[0], dtype=jnp.int32)[None, :] <= position[:, None]) & (
                seg_keys[None, :] == seg[:, None]
            )
            mixed, lse = attend_far(q, k, v, allowed)

        third_line = gather_line(third_pack, o, mixed)
        third_sides = gather_sides(third_line)
        second_sides = [after(t, mixed) for t in second_sides]
        second_all = gather_rest(second_line, second_sides, i, x).reshape(width, -1)
        second_other = swap(second_all)
        third_all = gather_rest(third_line, third_sides, i, x).reshape(hidden // 2, width)
        third_other = swap(third_all)
        ups = (second_all[:, : hidden // 2], second_other[:, : hidden // 2])
        downs = (third_all, third_other)
        w_out = in_order(second_all[:, hidden // 2 :], second_other[:, hidden // 2 :], 1)
        mixed_other = swap(lax.dynamic_slice_in_dim(mixed, (1 - core) * own, own, 0))
        mixed_own = in_order(lax.dynamic_slice_in_dim(mixed, core * own, own, 0), mixed_other, 1)
        mixed_own = after(mixed_own, third_line)
        midway = x_own + jnp.dot(mixed_own, w_out, preferred_element_type=f32) + b_out
        xhat2, inverse2 = standardize(midway)
        hidden2 = (xhat2 * gain2 + shift2).astype(bf16)
        activs, slopes = [], []
        result = midway + b_down
        for n in range(2):
            b_up = jnp.where(core == n, b_up_all[:1], b_up_all[1:])
            pre = jnp.dot(hidden2, ups[n], preferred_element_type=f32) + b_up
            square = pre * pre
            bend = jnp.tanh(GELU_A * pre * (1.0 + GELU_B * square))
            rise = 0.5 * (1.0 + bend)
            activs.append((pre * rise).astype(bf16))
            slope = rise + 0.5 * pre * (1.0 - bend * bend) * (GELU_A * (1.0 + 3.0 * GELU_B * square))
            slopes.append(slope.astype(bf16))
            result += jnp.dot(activs[n], downs[n], preferred_element_type=f32)
        grad_low = to_chips(after(cotangent, *third_sides)).reshape(own, width)
        result = result.astype(bf16)

        grad_out = grad_low.astype(f32)
        d_down_b = jnp.sum(grad_out, axis=0, keepdims=True)
        d_pres = [None, None]
        d_downs = [None, None]
        d_ups = [None, None]
        for n in (1, 0):
            d_downs[n] = dot(activs[n], grad_low, 0, 0).astype(bf16)
        d_down_other = swap(d_downs[1])
        grad_next = after(grad_low, *d_downs)
        for n in (1, 0):
            d_pres[n] = (dot(grad_next, downs[n], 1, 1) * slopes[n].astype(f32)).astype(bf16)
            d_ups[n] = dot(hidden2, d_pres[n], 0, 0).astype(bf16)
        d_up_other = swap(d_ups[1])
        d_down_sum = (after(d_downs[0], d_pres[1]).astype(f32) + d_down_other.astype(f32)).astype(bf16)
        down_state = reduce_far(d_down_sum.reshape(outer, inner, X, deep // 2 // X, width), i, x)
        d_pre = after(d_pres[0], *down_state[1])
        d_hidden2 = dot(d_pre, ups[0], 1, 1) + dot(d_pres[1], ups[1], 1, 1)
        d_up_bs = [jnp.sum(t.astype(f32), axis=0, keepdims=True) for t in d_pres]
        d_norm2, d_gain2, d_shift2 = norm_backward(d_hidden2, xhat2, inverse2, gain2)
        d_mid = grad_out + d_norm2
        d_branch = d_mid.astype(bf16)
        d_mixed = dot(d_branch, w_out, 1, 1).astype(bf16)
        d_mixed_other = swap(lax.dynamic_slice_in_dim(d_mixed, (1 - core) * half, half, 1))
        d_out = dot(mixed_own, d_branch, 0, 0).astype(bf16)
        d_out_b = jnp.sum(d_branch.astype(f32), axis=0, keepdims=True)
        d_out_other = swap(lax.dynamic_slice_in_dim(d_out, (1 - core) * half, half, 1))
        d_second = jnp.concatenate(
            [
                (d_ups[0].astype(f32) + d_up_other.astype(f32)).astype(bf16),
                (lax.dynamic_slice_in_dim(d_out, core * half, half, 1).astype(f32) + d_out_other.astype(f32)).astype(bf16),
            ],
            axis=1,
        )
        second_state = reduce_far(d_second.reshape(outer, inner, X, slim, -1), i, x)

        d_heads = in_order(lax.dynamic_slice_in_dim(d_mixed, core * half, half, 1), d_mixed_other, 0)
        down_plane = reduce_sides(down_state, i, x, (d_pres[0],), (d_mixed,))
        d_heads = after(d_heads, d_second, down_plane)
        if chips == 1:
            dq, dk, dv = attend_back(q, k, v, d_heads, lse, seg_col, seg_row)
        else:
            dq, dk, dv = attend_far_back(q, k, v, d_heads, lse, allowed)
            dk, dv = (
                lax.psum_scatter(
                    t.astype(bf16), "fsdp", scatter_dimension=0, tiled=True, axis_index_groups=groups
                )
                for t in (dk, dv)
            )
            dq = dq.astype(bf16)
        output = to_blocks(result, dq)
        dq = after(dq, *second_state[1])
        d_down_red = reduce_line(down_plane, o, dq)
        d_joined = jnp.concatenate([dq, dk, dv], axis=1)
        d_w_heads = dot(hidden1, d_joined, 0, 0)
        d_hidden1 = dot(d_joined, w_heads, 1, 1)
        second_plane = reduce_sides(second_state, i, x, (dq,), (d_w_heads,))
        d_second_red = reduce_line(second_plane, o)
        d_hidden1_other = swap(lax.dynamic_slice_in_dim(d_hidden1, (1 - core) * own, own, 0).astype(bf16))
        d_hidden1 = lax.dynamic_slice_in_dim(d_hidden1, core * own, own, 0) + d_hidden1_other.astype(f32)
        xhat1, inverse1 = standardize(x_own)
        d_norm1, d_gain1, d_shift1 = norm_backward(d_hidden1, xhat1, inverse1, gain1)
        d_inputs = to_blocks((d_mid + d_norm1).astype(bf16))

        d_bias = jnp.sum(d_joined.astype(f32), axis=0, keepdims=True)

        d_small = pack_small(
            core,
            (d_out_b, d_gain1, d_shift1, d_down_b, d_gain2, d_shift2),
            d_bias,
            d_up_bs[0],
            d_up_bs[1],
            F,
            slim * wide,
        ).reshape(F, 1, slim, wide * 128)
        d_small = jnp.pad(d_small, ((0, 0), (0, X - 1), (0, 0), (0, 0))).reshape(width, wide * 128)
        d_first = jnp.concatenate([d_w_heads, d_small], axis=1).astype(bf16)
        first_state = reduce_far(d_first.reshape(outer, inner, X, slim, lanes + wide * 128), i, x)
        d_first_red = reduce_line(reduce_sides(first_state, i, x, (), ()), o)

        d_first_red, d_second_red, d_down_red = [gather_x(t, x) for t in (d_first_red, d_second_red, d_down_red)]
        first_o, second_o, down_o = [swap(t) for t in (d_first_red, d_second_red, d_down_red)]
        cols = half
        pieces = []
        for n in range(3):
            sl = slice(n * cols, (n + 1) * cols)
            pieces.append(in_order(d_first_red[:, sl], first_o[:, sl], 1))
        d_qkv_w = jnp.concatenate(pieces, axis=1).astype(f32)
        small_sum = d_first_red[:slim, lanes:].astype(f32) + first_o[:slim, lanes:].astype(f32)
        small_sum = small_sum.reshape(slim * wide, 128)
        vec = [small_sum[n, :part] for n in range(8)]
        d_up_b = small_sum[8 : 8 + deep_rows].reshape(deep_rows * 128)[:deep]
        d_up_w = weave(core, d_second_red[:, : hidden // 2], second_o[:, : hidden // 2], F)
        d_out_w = in_order(d_second_red[:, hidden // 2 :], second_o[:, hidden // 2 :], 1).astype(f32)
        d_down_w = in_order(d_down_red, down_o, 0).astype(f32)
        return (
            output,
            d_inputs,
            d_qkv_w,
            vec[0],
            vec[1],
            d_out_w,
            vec[2],
            vec[3],
            vec[4],
            d_up_w,
            d_up_b,
            d_down_w,
            vec[5],
            vec[6],
            vec[7],
        )

    return local


def solution(mesh):
    in_specs = (
        P("dp", "fsdp", None),
        P("dp", "fsdp"),
        P("dp", "fsdp", None),
        P("fsdp", None),
        P("fsdp"),
        P("fsdp"),
        P("fsdp", None),
        P("fsdp"),
        P("fsdp"),
        P("fsdp"),
        P("fsdp", None),
        P("fsdp"),
        P("fsdp", None),
        P("fsdp"),
        P("fsdp"),
        P("fsdp"),
    )
    out_specs = (
        P("dp", "fsdp", None),
        P("dp", "fsdp", None),
        P("fsdp", None),
        P("fsdp"),
        P("fsdp"),
        P("fsdp", None),
        P("fsdp"),
        P("fsdp"),
        P("fsdp"),
        P("fsdp", None),
        P("fsdp"),
        P("fsdp", None),
        P("fsdp"),
        P("fsdp"),
        P("fsdp"),
    )
    local = build(mesh.shape["dp"], mesh.shape["fsdp"])
    return jax.shard_map(local, mesh=mesh, in_specs=in_specs, out_specs=out_specs, check_vma=False)
```

```python
import jax
import jax.numpy as jnp
from jax import lax
from jax.experimental import pallas as pl
from jax.experimental.pallas import tpu as pltpu
from jax.sharding import PartitionSpec as P

HEAD_DIM = 64
NEG = -1e30
GELU_A = 0.7978845608
GELU_B = 0.044715
f32 = jnp.float32
bf16 = jnp.bfloat16


def dot(a, b, ca, cb):
    return lax.dot_general(a, b, (((ca,), (cb,)), ((), ())), preferred_element_type=f32)


def block_scores(k, q_block, seg_col, seg_row, start, rows):
    parts = []
    if start:
        s = dot(k[:start], q_block, 1, 1)
        parts.append(jnp.where(seg_col[:start] == seg_row, s, NEG))
    s = dot(k[start : start + rows], q_block, 1, 1)
    row = lax.broadcasted_iota(jnp.int32, s.shape, 0)
    col = lax.broadcasted_iota(jnp.int32, s.shape, 1)
    parts.append(jnp.where((seg_col[start : start + rows] == seg_row) & (row <= col), s, NEG))
    return parts


def attend_kernel(q_ref, k_ref, v_ref, seg_col_ref, seg_row_ref, o_ref, lse_ref, *, rows):
    length = k_ref.shape[0]
    for head in range(2):
        lanes = slice(head * HEAD_DIM, (head + 1) * HEAD_DIM)
        k = k_ref[:, lanes]
        v_t = v_ref[:, lanes].T
        for start in range(0, length, rows):
            stop = start + rows
            parts = block_scores(
                k, q_ref[start:stop, lanes], seg_col_ref, seg_row_ref[:, start:stop], start, rows
            )
            top = jnp.max(parts[-1], axis=0, keepdims=True)
            if start:
                top = jnp.maximum(top, jnp.max(parts[0], axis=0, keepdims=True))
            expo = [jnp.exp(s - top) for s in parts]
            total = sum(jnp.sum(e, axis=0, keepdims=True) for e in expo)
            mixed = dot(v_t[:, start:stop], expo[-1].astype(bf16), 1, 0)
            if start:
                mixed += dot(v_t[:, :start], expo[0].astype(bf16), 1, 0)
            o_ref[start:stop, lanes] = (mixed / total).T.astype(bf16)
            lse_ref[head : head + 1, start:stop] = top + jnp.log(total)


def attend_back_kernel(
    q_ref, k_ref, v_ref, do_ref, lse_ref, seg_col_ref, seg_row_ref, dq_ref, dk_ref, dv_ref, dk_acc, dv_acc, *, rows
):
    length = k_ref.shape[0]
    scale = HEAD_DIM ** (-0.5)
    for head in range(2):
        lanes = slice(head * HEAD_DIM, (head + 1) * HEAD_DIM)
        k = k_ref[:, lanes]
        v = v_ref[:, lanes]
        k_t = k.T
        for start in range(length - rows, -1, -rows):
            stop = start + rows
            q_block = q_ref[start:stop, lanes]
            do_block = do_ref[start:stop, lanes]
            lse = lse_ref[head : head + 1, start:stop]
            parts = block_scores(k, q_block, seg_col_ref, seg_row_ref[:, start:stop], start, rows)
            spans = [(0, start), (start, stop)] if start else [(start, stop)]
            probs = [jnp.exp(s - lse) for s in parts]
            d_probs = [dot(v[lo:hi], do_block, 1, 1) for lo, hi in spans]
            delta = sum(jnp.sum(p * d, axis=0, keepdims=True) for p, d in zip(probs, d_probs))
            dq_t = 0.0
            for (lo, hi), p, d in zip(spans, probs, d_probs):
                ds = (p * (d - delta)).astype(bf16)
                dq_t += dot(k_t[:, lo:hi], ds, 1, 0)
                dk_part = dot(ds, q_block, 1, 0)
                dv_part = dot(p.astype(bf16), do_block, 1, 0)
                if stop == length:
                    dk_acc[lo:hi, :] = dk_part
                    dv_acc[lo:hi, :] = dv_part
                else:
                    dk_acc[lo:hi, :] += dk_part
                    dv_acc[lo:hi, :] += dv_part
            dq_ref[start:stop, lanes] = (dq_t * scale).T.astype(bf16)
        dk_ref[:, lanes] = dk_acc[...].astype(bf16)
        dv_ref[:, lanes] = dv_acc[...].astype(bf16)


def attend(q, k, v, seg_col, seg_row):
    length, width = q.shape
    pairs = width // 128
    wide = pl.BlockSpec((length, 128), lambda p: (0, p))
    return pl.pallas_call(
        lambda *refs: attend_kernel(*refs, rows=min(256, length)),
        out_shape=(
            jax.ShapeDtypeStruct((length, width), bf16),
            jax.ShapeDtypeStruct((pairs, 8, length), f32),
        ),
        grid=(pairs,),
        in_specs=[
            wide,
            wide,
            wide,
            pl.BlockSpec((length, 1), lambda p: (0, 0)),
            pl.BlockSpec((1, length), lambda p: (0, 0)),
        ],
        out_specs=(wide, pl.BlockSpec((None, 8, length), lambda p: (p, 0, 0))),
        compiler_params=pltpu.CompilerParams(vmem_limit_bytes=48 * 1024 * 1024),
        cost_estimate=pl.CostEstimate(
            flops=28 * length * length * width, bytes_accessed=8 * length * width, transcendentals=length * length * 4
        ),
        name="attend",
    )(q, k, v, seg_col, seg_row)


def attend_back(q, k, v, d_mixed, lse, seg_col, seg_row):
    length, width = q.shape
    pairs = width // 128
    wide = pl.BlockSpec((length, 128), lambda p: (0, p))
    return pl.pallas_call(
        lambda *refs: attend_back_kernel(*refs, rows=min(256, length)),
        out_shape=(jax.ShapeDtypeStruct((length, width), bf16),) * 3,
        grid=(pairs,),
        in_specs=[
            wide,
            wide,
            wide,
            wide,
            pl.BlockSpec((None, 8, length), lambda p: (p, 0, 0)),
            pl.BlockSpec((length, 1), lambda p: (0, 0)),
            pl.BlockSpec((1, length), lambda p: (0, 0)),
        ],
        out_specs=(wide, wide, wide),
        scratch_shapes=[pltpu.VMEM((length, HEAD_DIM), f32)] * 2,
        compiler_params=pltpu.CompilerParams(vmem_limit_bytes=48 * 1024 * 1024),
        cost_estimate=pl.CostEstimate(
            flops=50 * length * length * width, bytes_accessed=16 * length * width, transcendentals=length * length * 4
        ),
        name="attend_back",
    )(q, k, v, d_mixed, lse, seg_col, seg_row)


def split_heads(t):
    return t.reshape(t.shape[0], -1, HEAD_DIM).transpose(1, 0, 2)


def join_heads(t):
    return t.transpose(1, 0, 2).reshape(t.shape[1], -1)


def attend_far(q, k, v, allowed):
    def one(item):
        qh, kh, vh = item
        s = jnp.where(allowed, dot(qh, kh, 1, 1), NEG)
        top = jnp.max(s, axis=-1, keepdims=True)
        e = jnp.exp(s - top)
        total = jnp.sum(e, axis=-1, keepdims=True)
        return dot((e / total).astype(bf16), vh, 1, 0), (top + jnp.log(total))[:, 0]

    mixed, lse = lax.map(one, (split_heads(q), split_heads(k), split_heads(v)))
    return join_heads(mixed).astype(bf16), lse


def attend_far_back(q, k, v, d_mixed, lse, allowed):
    def one(item):
        qh, kh, vh, dh, l = item
        p = jnp.exp(jnp.where(allowed, dot(qh, kh, 1, 1), NEG) - l[:, None])
        dp = dot(dh, vh, 1, 1)
        ds = (p * (dp - jnp.sum(p * dp, axis=-1, keepdims=True))).astype(bf16)
        return (
            dot(ds, kh, 1, 0) * HEAD_DIM ** (-0.5),
            dot(ds, qh, 0, 0),
            dot(p.astype(bf16), dh, 0, 0),
        )

    grads = lax.map(one, (split_heads(q), split_heads(k), split_heads(v), split_heads(d_mixed), lse))
    return tuple(join_heads(g) for g in grads)


def place(pieces, indices, shape, spans):
    table = jnp.stack([jnp.asarray(v, jnp.int32) for index in indices for v in index])
    offsets = []
    for index in indices:
        offsets.append(sum(len(t) for t in indices[: len(offsets)]))

    def kernel(table_ref, *refs):
        out_ref, sems = refs[len(pieces)], refs[len(pieces) + 1]
        copies = []
        for n, span in enumerate(spans):
            spot = tuple(table_ref[offsets[n] + m] for m in range(len(indices[n])))
            target = out_ref.at[spot] if span is None else out_ref.at[(span,) + spot]
            copies.append(pltpu.make_async_copy(refs[n], target, sems.at[n]))
        for copy in copies:
            copy.start()
        for copy in copies:
            copy.wait()

    size = 2
    for extent in shape:
        size *= extent
    return pl.pallas_call(
        kernel,
        out_shape=jax.ShapeDtypeStruct(shape, pieces[0].dtype),
        in_specs=[pl.BlockSpec(memory_space=pltpu.SMEM)] + [pl.BlockSpec(memory_space=pl.ANY)] * len(pieces),
        out_specs=pl.BlockSpec(memory_space=pltpu.VMEM),
        scratch_shapes=[pltpu.SemaphoreType.DMA((len(pieces),))],
        compiler_params=pltpu.CompilerParams(vmem_limit_bytes=2 * size + (8 << 20)),
        cost_estimate=pl.CostEstimate(flops=0, bytes_accessed=2 * size, transcendentals=0),
        name="place",
    )(table, *pieces)


def after(a, *others):
    return lax.optimization_barrier((a,) + others)[0] if others else a


def unpack_small(small, part, deep):
    count = small.shape[0]

    def kernel(in_ref, vec_ref, up_ref):
        for f in range(count):
            rows = in_ref[f].astype(f32)
            vec_ref[:, f * part : (f + 1) * part] = rows[:8, :part]
            for row in range(-(-deep // 128)):
                size = min(128, deep - row * 128)
                start = f * deep + row * 128
                up_ref[:, start : start + size] = rows[8 + row : 9 + row, :size]

    return pl.pallas_call(
        kernel,
        out_shape=(
            jax.ShapeDtypeStruct((8, count * part), f32),
            jax.ShapeDtypeStruct((1, count * deep), f32),
        ),
        name="unpack_small",
    )(small)


def pack_small(core, rows_in, d_bias, d_up):
    width = rows_in[0].shape[1]
    half, more = width // 2, d_up.shape[1] // width
    core = jnp.reshape(core, (1,)).astype(jnp.int32)

    def kernel(core_ref, bias_ref, up_ref, *refs):
        out_ref = refs[-1]
        first = core_ref[0] == 0
        none = jnp.zeros((1, half), f32)
        for n, lo in enumerate((0, 2 * half)):
            mine = bias_ref[:, lo : lo + half]
            out_ref[n : n + 1, :half] = jnp.where(first, mine, none)
            out_ref[n : n + 1, half:] = jnp.where(first, none, mine)
        for n in range(6):
            out_ref[2 + n : 3 + n, :] = refs[n][...]
        for n in range(more):
            out_ref[8 + n : 9 + n, :] = up_ref[:, n * width : (n + 1) * width]

    return pl.pallas_call(
        kernel,
        out_shape=jax.ShapeDtypeStruct((8 + more, width), f32),
        in_specs=[pl.BlockSpec(memory_space=pltpu.SMEM)] + [pl.BlockSpec(memory_space=pltpu.VMEM)] * 8,
        name="pack_small",
    )(core, d_bias, d_up, *rows_in)


def standardize(values):
    centered = values - jnp.mean(values, axis=-1, keepdims=True)
    spread = jnp.mean(centered * centered, axis=-1, keepdims=True)
    inverse = lax.rsqrt(spread + 1e-05)
    return centered * inverse, inverse


def norm_backward(grad, xhat, inverse, gain):
    dz = grad * gain
    d_in = inverse * (
        dz - jnp.mean(dz, axis=-1, keepdims=True) - xhat * jnp.mean(dz * xhat, axis=-1, keepdims=True)
    )
    return d_in, jnp.sum(grad * xhat, axis=0, keepdims=True), jnp.sum(grad, axis=0, keepdims=True)


def build(dp_size, fsdp_size):
    F = fsdp_size
    X = dp_size // 2
    inner = 2 ** ((F.bit_length() - 1) // 2)
    outer = F // inner

    def swap(a):
        return lax.ppermute(a, "dp", [(d, d ^ 1) for d in range(dp_size)])

    def along(a, step_outer, step_inner):
        perm = []
        for o in range(outer):
            for i in range(inner):
                src = ((o + step_outer) % outer) * inner + (i + step_inner) % inner
                perm.append((src, o * inner + i))
        return lax.ppermute(a, "fsdp", perm)

    def across(a, step):
        return lax.ppermute(a, "dp", [((d + 2 * step) % dp_size, d) for d in range(dp_size)])

    def gather_line(a, o, *late):
        pieces = [after(a, *late)] + [along(a, step, 0) for step in range(1, outer)]
        return place(
            pieces, [((o + step) % outer,) for step in range(outer)], (outer,) + a.shape, [None] * outer
        )

    cube = inner == 2 and X == 2 and outer % 2 == 0
    cut = outer // 2

    def gather_sides(line):
        return (across(line, 1), along(line, 0, 1)) if cube else ()

    def gather_rest(line, sides, i, x):
        shape = (outer, inner, X) + line.shape[1:]
        if cube:
            by_x, by_y = sides
            low, high = across(by_y[:cut], 1), along(by_x[cut:], 0, 1)
            return place(
                [line, by_x, by_y, low, high],
                [(i, x), (i, 1 - x), (1 - i, x), (1 - i, 1 - x), (1 - i, 1 - x)],
                shape,
                [slice(None)] * 3 + [slice(0, cut), slice(cut, outer)],
            )
        plane = jnp.zeros((outer, X) + line.shape[1:], line.dtype)
        for step in range(X):
            plane = lax.dynamic_update_index_in_dim(plane, across(line, step) if step else line, (x + step) % X, 1)
        both = jnp.zeros(shape, line.dtype)
        for step in range(inner):
            both = lax.dynamic_update_index_in_dim(both, along(plane, 0, step) if step else plane, (i + step) % inner, 1)
        return both

    def pick(a, index, axis):
        return lax.dynamic_index_in_dim(a, index, axis, keepdims=False)

    def part(a, di, dx, i, x):
        return pick(pick(a, i ^ di, 1), x ^ dx, 1)

    def reduce_far(a, i, x):
        if not cube:
            return a, ()
        far = part(a, 1, 1, i, x)
        low, high = lax.optimization_barrier((far[:cut], far[cut:]))
        return a, (along(low, 0, 1), across(high, 1))

    def reduce_sides(state, i, x, late_far, late_sides):
        a, far = state
        if cube:
            here = after(a, *late_far)
            to_x, to_y = part(here, 0, 1, i, x), part(here, 1, 0, i, x)
            from_y, from_x = far
            to_x = jnp.concatenate([(to_x[:cut].astype(f32) + from_y.astype(f32)).astype(bf16), to_x[cut:]])
            to_y = jnp.concatenate([to_y[:cut], (to_y[cut:].astype(f32) + from_x.astype(f32)).astype(bf16)])
            to_x, to_y = lax.optimization_barrier((to_x, to_y))
            own = part(after(a, *late_sides), 0, 0, i, x)
            return (own.astype(f32) + across(to_x, 1).astype(f32) + along(to_y, 0, 1).astype(f32)).astype(bf16)
        total = pick(a, x, 2).astype(f32)
        for step in range(1, X):
            total += across(pick(a, (x + X - step) % X, 2), step).astype(f32)
        a = total.astype(bf16)
        total = pick(a, i, 1).astype(f32)
        for step in range(1, inner):
            total += along(pick(a, (i + inner - step) % inner, 1), 0, step).astype(f32)
        return total.astype(bf16)

    def reduce_line(a, o, *late):
        terms = lax.optimization_barrier(tuple(pick(a, (o + outer - step) % outer, 0) for step in range(1, outer)))
        total = pick(after(a, *late), o, 0).astype(f32)
        for step in range(1, outer):
            total += along(terms[step - 1], step, 0).astype(f32)
        return total.astype(bf16)

    def gather_x(a, x):
        if X == 2:
            other = across(a, 1)
            return jnp.concatenate([jnp.where(x == 0, a, other), jnp.where(x == 0, other, a)], axis=0)
        full = jnp.zeros((X,) + a.shape, a.dtype)
        for step in range(X):
            full = lax.dynamic_update_index_in_dim(full, across(a, step) if step else a, (x + step) % X, 0)
        return full.reshape((X * a.shape[0],) + a.shape[1:])

    def local(
        inputs,
        segments,
        cotangent,
        qkv_weight,
        query_bias,
        value_bias,
        out_weight,
        out_bias,
        norm1_gain,
        norm1_shift,
        up_weight,
        up_bias,
        down_weight,
        down_bias,
        norm2_gain,
        norm2_shift,
    ):
        seqs, block, width = inputs.shape
        hidden = up_weight.shape[1]
        chips = F // (2 * seqs)
        per_core = F // chips // 2
        own = per_core * block
        half = width // 2
        part = width // F
        deep = hidden // F
        core = lax.axis_index("dp") % 2
        x = lax.axis_index("dp") // 2
        f = lax.axis_index("fsdp")
        o, i = f // inner, f % inner
        is_first = core == 0

        def route(k, back):
            perm = []
            for plane in range(X):
                for c in range(2):
                    for b in range(F):
                        t = b % per_core
                        to_core = (b // per_core) % 2
                        to_chip = (c * seqs + (t ^ k)) * chips + b // (2 * per_core)
                        pair = ((plane * 2 + c) * F + b, (plane * 2 + to_core) * F + to_chip)
                        perm.append(pair[::-1] if back else pair)
            return perm

        slot = f % per_core
        seq_here = (f // chips) % seqs

        def to_chips(a, *late):
            got = [
                lax.ppermute(
                    lax.dynamic_index_in_dim(a, slot ^ k, 0, keepdims=False), ("dp", "fsdp"), route(k, False)
                )
                for k in range(seqs)
            ]
            got[0] = after(got[0], *late)
            got = jnp.stack(got)
            return jnp.concatenate(
                [lax.dynamic_index_in_dim(got, t ^ seq_here, 0) for t in range(per_core)], axis=0
            )

        def to_blocks(a, *late):
            a = a.reshape(per_core, block, width)
            got = [
                lax.ppermute(
                    lax.dynamic_index_in_dim(a, seq_here ^ k, 0, keepdims=False), ("dp", "fsdp"), route(k, True)
                )
                for k in range(seqs)
            ]
            got[0] = after(got[0], *late)
            got = jnp.stack(got)
            return jnp.concatenate(
                [lax.dynamic_index_in_dim(got, s ^ slot, 0) for s in range(seqs)], axis=0
            )

        def in_order(mine, other, axis):
            return jnp.concatenate(
                [jnp.where(is_first, mine, other), jnp.where(is_first, other, mine)], axis=axis
            )

        heads_w = jnp.concatenate(
            [lax.dynamic_slice_in_dim(qkv_weight, n * width + core * half, half, 1) for n in range(3)], axis=1
        )
        lanes = heads_w.shape[1]

        def x_rows(a):
            rows = a.shape[0] // X
            return lax.dynamic_slice_in_dim(a, x * rows, rows, 0)

        slim = part // X
        deep_rows = -(-deep // 128)
        wide = -(-(8 + deep_rows) // slim)
        singles = (query_bias, value_bias, out_bias, norm1_gain, norm1_shift, down_bias, norm2_gain, norm2_shift)
        row = lax.broadcasted_iota(jnp.int32, (slim * wide, 128), 0)
        small = jnp.pad(
            jnp.pad(up_bias, (0, deep_rows * 128 - deep)).reshape(deep_rows, 128),
            ((8, slim * wide - 8 - deep_rows), (0, 0)),
        )
        for n, vector in enumerate(singles):
            small = jnp.where(row == n, jnp.pad(vector, (0, 128 - part))[None, :], small)
        first_line = gather_line(
            jnp.concatenate([x_rows(heads_w), small.reshape(slim, wide * 128)], axis=1), o
        )
        first_sides = gather_sides(first_line)

        seg_row_own = jnp.pad(segments.astype(bf16)[:, None, :], ((0, 0), (0, 7), (0, width - block)))
        tokens = to_chips(jnp.concatenate([inputs, seg_row_own], axis=1))
        tokens_other = swap(tokens)

        first_all = gather_rest(first_line, first_sides, i, x)
        w_heads = first_all.reshape(width, lanes + wide * 128)[:, :lanes]
        small_all = first_all[:, :, 0, :, lanes:].reshape(F, slim * wide, 128)
        vectors, b_up = unpack_small(small_all, part, deep)
        b_query, b_value, b_out, gain1, shift1, b_down, gain2, shift2 = [vectors[n : n + 1] for n in range(8)]

        def share(a):
            rows = a.shape[0] // dp_size
            return lax.dynamic_slice_in_dim(a, lax.axis_index("dp") * rows, rows, 0)

        second = jnp.concatenate([share(up_weight), share(out_weight)], axis=1)
        second = lax.all_gather(second, ("fsdp", "dp"), axis=0, tiled=True)
        w_up, w_out = second[:, :hidden], second[:, hidden:]
        w_down = lax.all_gather(share(down_weight), ("fsdp", "dp"), axis=0, tiled=True)

        x_own = tokens[:, :block].reshape(own, width).astype(f32)
        x_all = in_order(
            tokens[:, :block].reshape(own, width), tokens_other[:, :block].reshape(own, width), 0
        ).astype(f32)
        xhat_all, _ = standardize(x_all)
        hidden1 = (xhat_all * gain1 + shift1).astype(bf16)
        seg = in_order(
            tokens[:, block, :block].reshape(own), tokens_other[:, block, :block].reshape(own), 0
        ).astype(f32)
        joined = jnp.dot(hidden1, w_heads, preferred_element_type=f32)
        bq = jnp.where(is_first, b_query[:, :half], b_query[:, half:])
        bv = jnp.where(is_first, b_value[:, :half], b_value[:, half:])
        q = (joined[:, :half] + bq).astype(bf16) * bf16(HEAD_DIM ** (-0.5))
        k = joined[:, half : 2 * half].astype(bf16)
        v = (joined[:, 2 * half :] + bv).astype(bf16)
        cotangent = after(cotangent, q)
        if chips == 1:
            seg_col, seg_row = seg[:, None], seg[None, :]
            mixed, lse = attend(q, k, v, seg_col, seg_row)
        else:
            groups = [[g * chips + n for n in range(chips)] for g in range(F // chips)]
            k, v, seg_keys = (
                lax.all_gather(t, "fsdp", axis=0, tiled=True, axis_index_groups=groups) for t in (k, v, seg)
            )
            position = (f % chips) * 2 * own + jnp.arange(2 * own, dtype=jnp.int32)
            allowed = (jnp.arange(k.shape[0], dtype=jnp.int32)[None, :] <= position[:, None]) & (
                seg_keys[None, :] == seg[:, None]
            )
            mixed, lse = attend_far(q, k, v, allowed)

        mixed_other = swap(lax.dynamic_slice_in_dim(mixed, (1 - core) * own, own, 0))
        mixed_own = in_order(lax.dynamic_slice_in_dim(mixed, core * own, own, 0), mixed_other, 1)
        midway = x_own + jnp.dot(mixed_own, w_out, preferred_element_type=f32) + b_out
        xhat2, inverse2 = standardize(midway)
        hidden2 = (xhat2 * gain2 + shift2).astype(bf16)
        pre = jnp.dot(hidden2, w_up, preferred_element_type=f32) + b_up
        square = pre * pre
        bend = jnp.tanh(GELU_A * pre * (1.0 + GELU_B * square))
        rise = 0.5 * (1.0 + bend)
        activ = (pre * rise).astype(bf16)
        slope = rise + 0.5 * pre * (1.0 - bend * bend) * (GELU_A * (1.0 + 3.0 * GELU_B * square))
        slope = slope.astype(bf16)
        result = midway + b_down + jnp.dot(activ, w_down, preferred_element_type=f32)
        grad_low = to_chips(cotangent, activ).reshape(own, width)
        result = result.astype(bf16)

        grad_out = grad_low.astype(f32)
        d_down_b = jnp.sum(grad_out, axis=0, keepdims=True)

        def halves(a):
            a = a.reshape(F, 2, -1, a.shape[1])
            return pick(a, 1 - core, 1), pick(a, core, 1)

        def add(a, b):
            return (a.astype(f32) + b.astype(f32)).astype(bf16)

        d_down = dot(activ, grad_low, 0, 0).astype(bf16)
        give, keep = halves(d_down)
        d_down_other = swap(give)
        d_pre = (dot(after(grad_low, give), w_down, 1, 1) * slope.astype(f32)).astype(bf16)
        down_state = reduce_far(
            add(after(keep, d_pre), d_down_other).reshape(outer, inner, X, deep // 2 // X, width), i, x
        )
        d_up = dot(hidden2, d_pre, 0, 0).astype(bf16)
        give_up, keep_up = halves(d_up)
        d_up_other = swap(give_up)
        d_hidden2 = dot(after(d_pre, give_up), w_up, 1, 1)
        d_up_b = jnp.sum(d_pre.astype(f32), axis=0, keepdims=True)
        d_norm2, d_gain2, d_shift2 = norm_backward(d_hidden2, xhat2, inverse2, gain2)
        d_mid = grad_out + d_norm2
        d_branch = d_mid.astype(bf16)
        d_mixed = dot(d_branch, w_out, 1, 1).astype(bf16)
        d_mixed_other = swap(lax.dynamic_slice_in_dim(d_mixed, (1 - core) * half, half, 1))
        d_out = dot(mixed_own, d_branch, 0, 0).astype(bf16)
        d_out_b = jnp.sum(d_branch.astype(f32), axis=0, keepdims=True)
        give_out, keep_out = halves(d_out)
        d_second = jnp.concatenate([add(keep_up, d_up_other), add(keep_out, swap(give_out))], axis=2)
        second_state = reduce_far(d_second.reshape(outer, inner, X, slim // 2, -1), i, x)

        d_heads = in_order(lax.dynamic_slice_in_dim(d_mixed, core * half, half, 1), d_mixed_other, 0)
        d_heads = after(d_heads, d_second, *down_state[1])
        if chips == 1:
            dq, dk, dv = attend_back(q, k, v, d_heads, lse, seg_col, seg_row)
        else:
            dq, dk, dv = attend_far_back(q, k, v, d_heads, lse, allowed)
            dk, dv = (
                lax.psum_scatter(
                    t.astype(bf16), "fsdp", scatter_dimension=0, tiled=True, axis_index_groups=groups
                )
                for t in (dk, dv)
            )
            dq = dq.astype(bf16)
        output = to_blocks(result, dq)
        down_plane = reduce_sides(down_state, i, x, (d_heads,), ())
        dq = after(dq, down_plane, *second_state[1])
        d_joined = jnp.concatenate([dq, dk, dv], axis=1)
        d_w_heads = dot(hidden1, d_joined, 0, 0)
        d_first = d_w_heads.astype(bf16)
        first_state = reduce_far(d_first.reshape(outer, inner, X, slim, lanes), i, x)
        d_hidden1 = dot(d_joined, w_heads, 1, 1)
        d_hidden1_other = swap(lax.dynamic_slice_in_dim(d_hidden1, (1 - core) * own, own, 0).astype(bf16))
        d_hidden1 = lax.dynamic_slice_in_dim(d_hidden1, core * own, own, 0) + d_hidden1_other.astype(f32)
        xhat1, inverse1 = standardize(x_own)
        d_norm1, d_gain1, d_shift1 = norm_backward(d_hidden1, xhat1, inverse1, gain1)
        d_in = (d_mid + d_norm1).astype(bf16)
        d_inputs = to_blocks(d_in)
        d_down_red = reduce_line(down_plane, o, d_hidden1)
        second_plane = reduce_sides(second_state, i, x, (d_w_heads, *first_state[1]), (d_in,))
        first_plane = reduce_sides(first_state, i, x, (), (d_in,))
        second_plane, first_plane = lax.optimization_barrier((second_plane, first_plane))
        d_second_red = reduce_line(second_plane, o)
        d_first_red = reduce_line(first_plane, o)

        d_bias = jnp.sum(d_joined.astype(f32), axis=0, keepdims=True)

        d_gain1 = after(d_gain1, d_down_red)
        d_small = pack_small(core, (d_out_b, d_gain1, d_shift1, d_down_b, d_gain2, d_shift2), d_bias, d_up_b)
        d_small = after(d_small, second_plane)
        for axis, size in (("dp", dp_size), ("fsdp", F)):
            bit = 1
            while bit < size:
                d_small += lax.ppermute(d_small, axis, [(d, d ^ bit) for d in range(size)])
                bit *= 2
        d_first_red, d_second_red, d_down_red = lax.optimization_barrier((d_first_red, d_second_red, d_down_red))

        d_first_red, d_second_red, d_down_red = [gather_x(t, x) for t in (d_first_red, d_second_red, d_down_red)]
        first_o, second_o, down_o = [swap(t) for t in (d_first_red, d_second_red, d_down_red)]
        cols = half
        pieces = []
        for n in range(3):
            sl = slice(n * cols, (n + 1) * cols)
            pieces.append(in_order(d_first_red[:, sl], first_o[:, sl], 1))
        d_qkv_w = jnp.concatenate(pieces, axis=1).astype(f32)
        small_own = lax.dynamic_slice_in_dim(d_small[:8].reshape(8, F, part), f, 1, 1)
        vec = [small_own[n, 0] for n in range(8)]
        d_up_b = lax.dynamic_slice_in_dim(d_small[8:].reshape(hidden), f * deep, deep)
        d_second_w = in_order(d_second_red, second_o, 0).astype(f32)
        d_up_w, d_out_w = d_second_w[:, :hidden], d_second_w[:, hidden:]
        d_down_w = in_order(d_down_red, down_o, 0).astype(f32)
        return (
            output,
            d_inputs,
            d_qkv_w,
            vec[0],
            vec[1],
            d_out_w,
            vec[2],
            vec[3],
            vec[4],
            d_up_w,
            d_up_b,
            d_down_w,
            vec[5],
            vec[6],
            vec[7],
        )

    return local


def solution(mesh):
    in_specs = (
        P("dp", "fsdp", None),
        P("dp", "fsdp"),
        P("dp", "fsdp", None),
        P("fsdp", None),
        P("fsdp"),
        P("fsdp"),
        P("fsdp", None),
        P("fsdp"),
        P("fsdp"),
        P("fsdp"),
        P("fsdp", None),
        P("fsdp"),
        P("fsdp", None),
        P("fsdp"),
        P("fsdp"),
        P("fsdp"),
    )
    out_specs = (
        P("dp", "fsdp", None),
        P("dp", "fsdp", None),
        P("fsdp", None),
        P("fsdp"),
        P("fsdp"),
        P("fsdp", None),
        P("fsdp"),
        P("fsdp"),
        P("fsdp"),
        P("fsdp", None),
        P("fsdp"),
        P("fsdp", None),
        P("fsdp"),
        P("fsdp"),
        P("fsdp"),
    )
    local = build(mesh.shape["dp"], mesh.shape["fsdp"])
    return jax.shard_map(local, mesh=mesh, in_specs=in_specs, out_specs=out_specs, check_vma=False)
```

```python
import jax
import jax.numpy as jnp
from jax import lax
from jax.experimental import pallas as pl
from jax.experimental.pallas import tpu as pltpu
from jax.sharding import PartitionSpec as P

HEAD_DIM = 64
NEG = -1e30
GELU_A = 0.7978845608
GELU_B = 0.044715
f32 = jnp.float32
bf16 = jnp.bfloat16


def dot(a, b, ca, cb):
    return lax.dot_general(a, b, (((ca,), (cb,)), ((), ())), preferred_element_type=f32)


def block_scores(k, q_block, seg_col, seg_row, start, rows):
    parts = []
    if start:
        s = dot(k[:start], q_block, 1, 1)
        parts.append(jnp.where(seg_col[:start] == seg_row, s, NEG))
    s = dot(k[start : start + rows], q_block, 1, 1)
    row = lax.broadcasted_iota(jnp.int32, s.shape, 0)
    col = lax.broadcasted_iota(jnp.int32, s.shape, 1)
    parts.append(jnp.where((seg_col[start : start + rows] == seg_row) & (row <= col), s, NEG))
    return parts


def attend_kernel(q_ref, k_ref, v_ref, seg_col_ref, seg_row_ref, o_ref, lse_ref, *, rows):
    length = k_ref.shape[0]
    for head in range(2):
        lanes = slice(head * HEAD_DIM, (head + 1) * HEAD_DIM)
        k = k_ref[:, lanes]
        v_t = v_ref[:, lanes].T
        for start in range(0, length, rows):
            stop = start + rows
            parts = block_scores(
                k, q_ref[start:stop, lanes], seg_col_ref, seg_row_ref[:, start:stop], start, rows
            )
            top = jnp.max(parts[-1], axis=0, keepdims=True)
            if start:
                top = jnp.maximum(top, jnp.max(parts[0], axis=0, keepdims=True))
            expo = [jnp.exp(s - top) for s in parts]
            total = sum(jnp.sum(e, axis=0, keepdims=True) for e in expo)
            mixed = dot(v_t[:, start:stop], expo[-1].astype(bf16), 1, 0)
            if start:
                mixed += dot(v_t[:, :start], expo[0].astype(bf16), 1, 0)
            o_ref[start:stop, lanes] = (mixed / total).T.astype(bf16)
            lse_ref[head : head + 1, start:stop] = top + jnp.log(total)


def attend_back_kernel(
    q_ref, k_ref, v_ref, do_ref, lse_ref, seg_col_ref, seg_row_ref, dq_ref, dk_ref, dv_ref, dk_acc, dv_acc, *, rows
):
    length = k_ref.shape[0]
    scale = HEAD_DIM ** (-0.5)
    for head in range(2):
        lanes = slice(head * HEAD_DIM, (head + 1) * HEAD_DIM)
        k = k_ref[:, lanes]
        v = v_ref[:, lanes]
        k_t = k.T
        for start in range(length - rows, -1, -rows):
            stop = start + rows
            q_block = q_ref[start:stop, lanes]
            do_block = do_ref[start:stop, lanes]
            lse = lse_ref[head : head + 1, start:stop]
            parts = block_scores(k, q_block, seg_col_ref, seg_row_ref[:, start:stop], start, rows)
            spans = [(0, start), (start, stop)] if start else [(start, stop)]
            probs = [jnp.exp(s - lse) for s in parts]
            d_probs = [dot(v[lo:hi], do_block, 1, 1) for lo, hi in spans]
            delta = sum(jnp.sum(p * d, axis=0, keepdims=True) for p, d in zip(probs, d_probs))
            dq_t = 0.0
            for (lo, hi), p, d in zip(spans, probs, d_probs):
                ds = (p * (d - delta)).astype(bf16)
                dq_t += dot(k_t[:, lo:hi], ds, 1, 0)
                dk_part = dot(ds, q_block, 1, 0)
                dv_part = dot(p.astype(bf16), do_block, 1, 0)
                if stop == length:
                    dk_acc[lo:hi, :] = dk_part
                    dv_acc[lo:hi, :] = dv_part
                else:
                    dk_acc[lo:hi, :] += dk_part
                    dv_acc[lo:hi, :] += dv_part
            dq_ref[start:stop, lanes] = (dq_t * scale).T.astype(bf16)
        dk_ref[:, lanes] = dk_acc[...].astype(bf16)
        dv_ref[:, lanes] = dv_acc[...].astype(bf16)


def attend(q, k, v, seg_col, seg_row):
    length, width = q.shape
    pairs = width // 128
    wide = pl.BlockSpec((length, 128), lambda p: (0, p))
    return pl.pallas_call(
        lambda *refs: attend_kernel(*refs, rows=min(256, length)),
        out_shape=(
            jax.ShapeDtypeStruct((length, width), bf16),
            jax.ShapeDtypeStruct((pairs, 8, length), f32),
        ),
        grid=(pairs,),
        in_specs=[
            wide,
            wide,
            wide,
            pl.BlockSpec((length, 1), lambda p: (0, 0)),
            pl.BlockSpec((1, length), lambda p: (0, 0)),
        ],
        out_specs=(wide, pl.BlockSpec((None, 8, length), lambda p: (p, 0, 0))),
        compiler_params=pltpu.CompilerParams(vmem_limit_bytes=48 * 1024 * 1024),
        cost_estimate=pl.CostEstimate(
            flops=28 * length * length * width, bytes_accessed=8 * length * width, transcendentals=length * length * 4
        ),
        name="attend",
    )(q, k, v, seg_col, seg_row)


def attend_back(q, k, v, d_mixed, lse, seg_col, seg_row):
    length, width = q.shape
    pairs = width // 128
    wide = pl.BlockSpec((length, 128), lambda p: (0, p))
    return pl.pallas_call(
        lambda *refs: attend_back_kernel(*refs, rows=min(256, length)),
        out_shape=(jax.ShapeDtypeStruct((length, width), bf16),) * 3,
        grid=(pairs,),
        in_specs=[
            wide,
            wide,
            wide,
            wide,
            pl.BlockSpec((None, 8, length), lambda p: (p, 0, 0)),
            pl.BlockSpec((length, 1), lambda p: (0, 0)),
            pl.BlockSpec((1, length), lambda p: (0, 0)),
        ],
        out_specs=(wide, wide, wide),
        scratch_shapes=[pltpu.VMEM((length, HEAD_DIM), f32)] * 2,
        compiler_params=pltpu.CompilerParams(vmem_limit_bytes=48 * 1024 * 1024),
        cost_estimate=pl.CostEstimate(
            flops=50 * length * length * width, bytes_accessed=16 * length * width, transcendentals=length * length * 4
        ),
        name="attend_back",
    )(q, k, v, d_mixed, lse, seg_col, seg_row)


def split_heads(t):
    return t.reshape(t.shape[0], -1, HEAD_DIM).transpose(1, 0, 2)


def join_heads(t):
    return t.transpose(1, 0, 2).reshape(t.shape[1], -1)


def attend_far(q, k, v, allowed):
    def one(item):
        qh, kh, vh = item
        s = jnp.where(allowed, dot(qh, kh, 1, 1), NEG)
        top = jnp.max(s, axis=-1, keepdims=True)
        e = jnp.exp(s - top)
        total = jnp.sum(e, axis=-1, keepdims=True)
        return dot((e / total).astype(bf16), vh, 1, 0), (top + jnp.log(total))[:, 0]

    mixed, lse = lax.map(one, (split_heads(q), split_heads(k), split_heads(v)))
    return join_heads(mixed).astype(bf16), lse


def attend_far_back(q, k, v, d_mixed, lse, allowed):
    def one(item):
        qh, kh, vh, dh, l = item
        p = jnp.exp(jnp.where(allowed, dot(qh, kh, 1, 1), NEG) - l[:, None])
        dp = dot(dh, vh, 1, 1)
        ds = (p * (dp - jnp.sum(p * dp, axis=-1, keepdims=True))).astype(bf16)
        return (
            dot(ds, kh, 1, 0) * HEAD_DIM ** (-0.5),
            dot(ds, qh, 0, 0),
            dot(p.astype(bf16), dh, 0, 0),
        )

    grads = lax.map(one, (split_heads(q), split_heads(k), split_heads(v), split_heads(d_mixed), lse))
    return tuple(join_heads(g) for g in grads)


def place(pieces, indices, shape, spans):
    table = jnp.stack([jnp.asarray(v, jnp.int32) for index in indices for v in index])
    offsets = []
    for index in indices:
        offsets.append(sum(len(t) for t in indices[: len(offsets)]))

    def kernel(table_ref, *refs):
        out_ref, sems = refs[len(pieces)], refs[len(pieces) + 1]
        copies = []
        for n, span in enumerate(spans):
            spot = tuple(table_ref[offsets[n] + m] for m in range(len(indices[n])))
            target = out_ref.at[spot] if span is None else out_ref.at[(span,) + spot]
            copies.append(pltpu.make_async_copy(refs[n], target, sems.at[n]))
        for copy in copies:
            copy.start()
        for copy in copies:
            copy.wait()

    size = 2
    for extent in shape:
        size *= extent
    return pl.pallas_call(
        kernel,
        out_shape=jax.ShapeDtypeStruct(shape, pieces[0].dtype),
        in_specs=[pl.BlockSpec(memory_space=pltpu.SMEM)] + [pl.BlockSpec(memory_space=pl.ANY)] * len(pieces),
        out_specs=pl.BlockSpec(memory_space=pltpu.VMEM),
        scratch_shapes=[pltpu.SemaphoreType.DMA((len(pieces),))],
        compiler_params=pltpu.CompilerParams(vmem_limit_bytes=2 * size + (8 << 20)),
        cost_estimate=pl.CostEstimate(flops=0, bytes_accessed=2 * size, transcendentals=0),
        name="place",
    )(table, *pieces)


def unfold(pieces, indices, spans, grid, sizes, chunk):
    rows, cols = pieces[0].shape[1:]
    stacked = (cols - sum(sizes)) // chunk
    table = jnp.stack([jnp.asarray(v, jnp.int32) for index in indices for v in index])

    def kernel(table_ref, *refs):
        ins, outs, sems = refs[: len(pieces)], refs[len(pieces) : -1], refs[-1]
        copies = []
        for p, (source, span) in enumerate(zip(ins, spans)):
            spot = (span,) + tuple(table_ref[3 * p + m] for m in range(3))
            at = 0
            for out, size in zip(outs, sizes):
                copies.append((source.at[:, :, at : at + size], out.at[spot]))
                at += size
            for n in range(stacked):
                copies.append((source.at[:, :, at + n * chunk : at + (n + 1) * chunk], outs[-1].at[spot + (n,)]))
        copies = [pltpu.make_async_copy(a, b, sems.at[n]) for n, (a, b) in enumerate(copies)]
        for copy in copies:
            copy.start()
        for copy in copies:
            copy.wait()

    shapes = [grid + (rows, size) for size in sizes] + [grid + (stacked, rows, chunk)]
    return pl.pallas_call(
        kernel,
        out_shape=tuple(jax.ShapeDtypeStruct(shape, pieces[0].dtype) for shape in shapes),
        in_specs=[pl.BlockSpec(memory_space=pltpu.SMEM)] + [pl.BlockSpec(memory_space=pl.ANY)] * len(pieces),
        out_specs=tuple(pl.BlockSpec(memory_space=pltpu.VMEM) for _ in shapes),
        scratch_shapes=[pltpu.SemaphoreType.DMA((len(pieces) * (len(sizes) + stacked),))],
        compiler_params=pltpu.CompilerParams(vmem_limit_bytes=48 * 1024 * 1024),
        name="unfold",
    )(table, *pieces)


def fold(a, rows):
    lead = a.shape[:-2]
    a = a.reshape(lead + (-1, rows, a.shape[-1]))
    return jnp.concatenate([a[..., n, :, :] for n in range(a.shape[-3])], axis=-1)


def after(a, *others):
    return lax.optimization_barrier((a,) + others)[0] if others else a


def unpack_small(small, part, deep):
    count = small.shape[0]

    def kernel(in_ref, vec_ref, up_ref):
        for f in range(count):
            rows = in_ref[f].astype(f32)
            vec_ref[:, f * part : (f + 1) * part] = rows[:8, :part]
            for row in range(-(-deep // 128)):
                size = min(128, deep - row * 128)
                start = f * deep + row * 128
                up_ref[:, start : start + size] = rows[8 + row : 9 + row, :size]

    return pl.pallas_call(
        kernel,
        out_shape=(
            jax.ShapeDtypeStruct((8, count * part), f32),
            jax.ShapeDtypeStruct((1, count * deep), f32),
        ),
        name="unpack_small",
    )(small)


def pack_small(core, rows_in, d_bias, d_up):
    width = rows_in[0].shape[1]
    half, more = width // 2, d_up.shape[1] // width
    core = jnp.reshape(core, (1,)).astype(jnp.int32)

    def kernel(core_ref, bias_ref, up_ref, *refs):
        out_ref = refs[-1]
        first = core_ref[0] == 0
        none = jnp.zeros((1, half), f32)
        for n, lo in enumerate((0, 2 * half)):
            mine = bias_ref[:, lo : lo + half]
            out_ref[n : n + 1, :half] = jnp.where(first, mine, none)
            out_ref[n : n + 1, half:] = jnp.where(first, none, mine)
        for n in range(6):
            out_ref[2 + n : 3 + n, :] = refs[n][...]
        for n in range(more):
            out_ref[8 + n : 9 + n, :] = up_ref[:, n * width : (n + 1) * width]

    return pl.pallas_call(
        kernel,
        out_shape=jax.ShapeDtypeStruct((8 + more, width), f32),
        in_specs=[pl.BlockSpec(memory_space=pltpu.SMEM)] + [pl.BlockSpec(memory_space=pltpu.VMEM)] * 8,
        name="pack_small",
    )(core, d_bias, d_up, *rows_in)


def standardize(values):
    centered = values - jnp.mean(values, axis=-1, keepdims=True)
    spread = jnp.mean(centered * centered, axis=-1, keepdims=True)
    inverse = lax.rsqrt(spread + 1e-05)
    return centered * inverse, inverse


def norm_backward(grad, xhat, inverse, gain):
    dz = grad * gain
    d_in = inverse * (
        dz - jnp.mean(dz, axis=-1, keepdims=True) - xhat * jnp.mean(dz * xhat, axis=-1, keepdims=True)
    )
    return d_in, jnp.sum(grad * xhat, axis=0, keepdims=True), jnp.sum(grad, axis=0, keepdims=True)


def build(dp_size, fsdp_size):
    F = fsdp_size
    X = dp_size // 2
    inner = 2 ** ((F.bit_length() - 1) // 2)
    outer = F // inner

    def swap(a):
        return lax.ppermute(a, "dp", [(d, d ^ 1) for d in range(dp_size)])

    def along(a, step_outer, step_inner):
        perm = []
        for o in range(outer):
            for i in range(inner):
                src = ((o + step_outer) % outer) * inner + (i + step_inner) % inner
                perm.append((src, o * inner + i))
        return lax.ppermute(a, "fsdp", perm)

    def across(a, step):
        return lax.ppermute(a, "dp", [((d + 2 * step) % dp_size, d) for d in range(dp_size)])

    def gather_line(a, o, *late):
        pieces = [after(a, *late)] + [along(a, step, 0) for step in range(1, outer)]
        return place(
            pieces, [((o + step) % outer,) for step in range(outer)], (outer,) + a.shape, [None] * outer
        )

    cube = inner == 2 and X == 2 and outer % 2 == 0
    cut = outer // 2

    def gather_sides(line):
        return (across(line, 1), along(line, 0, 1)) if cube else ()

    def gather_rest(line, sides, i, x):
        shape = (outer, inner, X) + line.shape[1:]
        if cube:
            by_x, by_y = sides
            low, high = across(by_y[:cut], 1), along(by_x[cut:], 0, 1)
            return place(
                [line, by_x, by_y, low, high],
                [(i, x), (i, 1 - x), (1 - i, x), (1 - i, 1 - x), (1 - i, 1 - x)],
                shape,
                [slice(None)] * 3 + [slice(0, cut), slice(cut, outer)],
            )
        plane = jnp.zeros((outer, X) + line.shape[1:], line.dtype)
        for step in range(X):
            plane = lax.dynamic_update_index_in_dim(plane, across(line, step) if step else line, (x + step) % X, 1)
        both = jnp.zeros(shape, line.dtype)
        for step in range(inner):
            both = lax.dynamic_update_index_in_dim(both, along(plane, 0, step) if step else plane, (i + step) % inner, 1)
        return both

    def gather_apart(line, sides, i, x, core, sizes, chunk):
        grid = (outer, inner, X, 2)
        whole = slice(0, outer)
        if cube:
            by_x, by_y = sides
            low, high = across(by_y[:cut], 1), along(by_x[cut:], 0, 1)
            mine = [line, by_x, by_y, low, high]
            spots = [(i, x), (i, 1 - x), (1 - i, x), (1 - i, 1 - x), (1 - i, 1 - x)]
            spans = [whole] * 3 + [slice(0, cut), slice(cut, outer)]
        else:
            full = gather_rest(line, sides, i, x)
            mine = [full[:, n, m] for n in range(inner) for m in range(X)]
            spots = [(n, m) for n in range(inner) for m in range(X)]
            spans = [whole] * len(mine)
        indices = [spot + (core,) for spot in spots] + [spot + (1 - core,) for spot in spots]
        return unfold(mine + [swap(t) for t in mine], indices, spans * 2, grid, sizes, chunk)

    def pick(a, index, axis):
        return lax.dynamic_index_in_dim(a, index, axis, keepdims=False)

    def part(a, di, dx, i, x):
        return pick(pick(a, i ^ di, 1), x ^ dx, 1)

    def reduce_far(a, i, x):
        if not cube:
            return a, ()
        far = part(a, 1, 1, i, x)
        low, high = lax.optimization_barrier((far[:cut], far[cut:]))
        return a, (along(low, 0, 1), across(high, 1))

    def reduce_sides(state, i, x, late_far, late_sides):
        a, far = state
        if cube:
            here = after(a, *late_far)
            to_x, to_y = part(here, 0, 1, i, x), part(here, 1, 0, i, x)
            from_y, from_x = far
            to_x = jnp.concatenate([(to_x[:cut].astype(f32) + from_y.astype(f32)).astype(bf16), to_x[cut:]])
            to_y = jnp.concatenate([to_y[:cut], (to_y[cut:].astype(f32) + from_x.astype(f32)).astype(bf16)])
            to_x, to_y = lax.optimization_barrier((to_x, to_y))
            own = part(after(a, *late_sides), 0, 0, i, x)
            return (own.astype(f32) + across(to_x, 1).astype(f32) + along(to_y, 0, 1).astype(f32)).astype(bf16)
        total = pick(a, x, 2).astype(f32)
        for step in range(1, X):
            total += across(pick(a, (x + X - step) % X, 2), step).astype(f32)
        a = total.astype(bf16)
        total = pick(a, i, 1).astype(f32)
        for step in range(1, inner):
            total += along(pick(a, (i + inner - step) % inner, 1), 0, step).astype(f32)
        return total.astype(bf16)

    def reduce_line(a, o, *late):
        terms = lax.optimization_barrier(tuple(pick(a, (o + outer - step) % outer, 0) for step in range(1, outer)))
        total = pick(after(a, *late), o, 0).astype(f32)
        for step in range(1, outer):
            total += along(terms[step - 1], step, 0).astype(f32)
        return total.astype(bf16)

    def gather_x(a, x):
        if X == 2:
            other = across(a, 1)
            return jnp.concatenate([jnp.where(x == 0, a, other), jnp.where(x == 0, other, a)], axis=0)
        full = jnp.zeros((X,) + a.shape, a.dtype)
        for step in range(X):
            full = lax.dynamic_update_index_in_dim(full, across(a, step) if step else a, (x + step) % X, 0)
        return full.reshape((X * a.shape[0],) + a.shape[1:])

    def local(
        inputs,
        segments,
        cotangent,
        qkv_weight,
        query_bias,
        value_bias,
        out_weight,
        out_bias,
        norm1_gain,
        norm1_shift,
        up_weight,
        up_bias,
        down_weight,
        down_bias,
        norm2_gain,
        norm2_shift,
    ):
        seqs, block, width = inputs.shape
        hidden = up_weight.shape[1]
        chips = F // (2 * seqs)
        per_core = F // chips // 2
        own = per_core * block
        half = width // 2
        part = width // F
        deep = hidden // F
        core = lax.axis_index("dp") % 2
        x = lax.axis_index("dp") // 2
        f = lax.axis_index("fsdp")
        o, i = f // inner, f % inner
        is_first = core == 0

        def route(k, back):
            perm = []
            for plane in range(X):
                for c in range(2):
                    for b in range(F):
                        t = b % per_core
                        to_core = (b // per_core) % 2
                        to_chip = (c * seqs + (t ^ k)) * chips + b // (2 * per_core)
                        pair = ((plane * 2 + c) * F + b, (plane * 2 + to_core) * F + to_chip)
                        perm.append(pair[::-1] if back else pair)
            return perm

        slot = f % per_core
        seq_here = (f // chips) % seqs

        def to_chips(a, *late):
            got = [
                lax.ppermute(
                    lax.dynamic_index_in_dim(a, slot ^ k, 0, keepdims=False), ("dp", "fsdp"), route(k, False)
                )
                for k in range(seqs)
            ]
            got[0] = after(got[0], *late)
            got = jnp.stack(got)
            return jnp.concatenate(
                [lax.dynamic_index_in_dim(got, t ^ seq_here, 0) for t in range(per_core)], axis=0
            )

        def to_blocks(a, *late):
            a = a.reshape(per_core, block, width)
            got = [
                lax.ppermute(
                    lax.dynamic_index_in_dim(a, seq_here ^ k, 0, keepdims=False), ("dp", "fsdp"), route(k, True)
                )
                for k in range(seqs)
            ]
            got[0] = after(got[0], *late)
            got = jnp.stack(got)
            return jnp.concatenate(
                [lax.dynamic_index_in_dim(got, s ^ slot, 0) for s in range(seqs)], axis=0
            )

        def in_order(mine, other, axis):
            return jnp.concatenate(
                [jnp.where(is_first, mine, other), jnp.where(is_first, other, mine)], axis=axis
            )

        heads_w = jnp.concatenate(
            [lax.dynamic_slice_in_dim(qkv_weight, n * width + core * half, half, 1) for n in range(3)], axis=1
        )
        lanes = heads_w.shape[1]

        def x_rows(a):
            rows = a.shape[0] // X
            return lax.dynamic_slice_in_dim(a, x * rows, rows, 0)

        slim = part // X
        deep_rows = -(-deep // 128)
        wide = -(-(8 + deep_rows) // slim)
        singles = (query_bias, value_bias, out_bias, norm1_gain, norm1_shift, down_bias, norm2_gain, norm2_shift)
        row = lax.broadcasted_iota(jnp.int32, (slim * wide, 128), 0)
        small = jnp.pad(
            jnp.pad(up_bias, (0, deep_rows * 128 - deep)).reshape(deep_rows, 128),
            ((8, slim * wide - 8 - deep_rows), (0, 0)),
        )
        for n, vector in enumerate(singles):
            small = jnp.where(row == n, jnp.pad(vector, (0, 128 - part))[None, :], small)
        first_line = gather_line(
            jnp.concatenate([x_rows(heads_w), small.reshape(slim, wide * 128)], axis=1), o
        )
        first_sides = gather_sides(first_line)

        seg_row_own = jnp.pad(segments.astype(bf16)[:, None, :], ((0, 0), (0, 7), (0, width - block)))
        tokens = to_chips(jnp.concatenate([inputs, seg_row_own], axis=1))
        tokens_other = swap(tokens)

        first_all = gather_rest(first_line, first_sides, i, x)
        w_heads = first_all.reshape(width, lanes + wide * 128)[:, :lanes]
        small_all = first_all[:, :, 0, :, lanes:].reshape(F, slim * wide, 128)
        vectors, b_up = unpack_small(small_all, part, deep)
        b_query, b_value, b_out, gain1, shift1, b_down, gain2, shift2 = [vectors[n : n + 1] for n in range(8)]

        def share(a):
            rows = a.shape[0] // dp_size
            return lax.dynamic_slice_in_dim(a, lax.axis_index("dp") * rows, rows, 0)

        thin = part // dp_size
        second_pack = after(
            jnp.concatenate([share(up_weight), share(out_weight), fold(share(down_weight), thin)], axis=1),
            tokens,
            *first_sides,
        )

        x_own = tokens[:, :block].reshape(own, width).astype(f32)
        x_all = in_order(
            tokens[:, :block].reshape(own, width), tokens_other[:, :block].reshape(own, width), 0
        ).astype(f32)
        xhat_all, _ = standardize(x_all)
        hidden1 = (xhat_all * gain1 + shift1).astype(bf16)
        seg = in_order(
            tokens[:, block, :block].reshape(own), tokens_other[:, block, :block].reshape(own), 0
        ).astype(f32)
        joined = jnp.dot(hidden1, w_heads, preferred_element_type=f32)
        bq = jnp.where(is_first, b_query[:, :half], b_query[:, half:])
        bv = jnp.where(is_first, b_value[:, :half], b_value[:, half:])
        q = (joined[:, :half] + bq).astype(bf16) * bf16(HEAD_DIM ** (-0.5))
        k = joined[:, half : 2 * half].astype(bf16)
        v = (joined[:, 2 * half :] + bv).astype(bf16)
        second_line = gather_line(second_pack, o, q)
        second_sides = gather_sides(second_line)
        q = after(q, second_line)
        if chips == 1:
            seg_col, seg_row = seg[:, None], seg[None, :]
            mixed, lse = attend(q, k, v, seg_col, seg_row)
        else:
            groups = [[g * chips + n for n in range(chips)] for g in range(F // chips)]
            k, v, seg_keys = (
                lax.all_gather(t, "fsdp", axis=0, tiled=True, axis_index_groups=groups) for t in (k, v, seg)
            )
            position = (f % chips) * 2 * own + jnp.arange(2 * own, dtype=jnp.int32)
            allowed = (jnp.arange(k.shape[0], dtype=jnp.int32)[None, :] <= position[:, None]) & (
                seg_keys[None, :] == seg[:, None]
            )
            mixed, lse = attend_far(q, k, v, allowed)

        cotangent = after(cotangent, second_line)
        second_sides = [after(t, mixed) for t in second_sides]
        w_up, w_out, w_down = gather_apart(second_line, second_sides, i, x, core, (hidden, width), width)
        w_up, w_out, w_down = w_up.reshape(width, hidden), w_out.reshape(width, width), w_down.reshape(hidden, width)
        mixed_other = swap(lax.dynamic_slice_in_dim(mixed, (1 - core) * own, own, 0))
        mixed_own = in_order(lax.dynamic_slice_in_dim(mixed, core * own, own, 0), mixed_other, 1)
        midway = x_own + jnp.dot(mixed_own, w_out, preferred_element_type=f32) + b_out
        xhat2, inverse2 = standardize(midway)
        hidden2 = (xhat2 * gain2 + shift2).astype(bf16)
        pre = jnp.dot(hidden2, w_up, preferred_element_type=f32) + b_up
        square = pre * pre
        bend = jnp.tanh(GELU_A * pre * (1.0 + GELU_B * square))
        rise = 0.5 * (1.0 + bend)
        activ = (pre * rise).astype(bf16)
        slope = rise + 0.5 * pre * (1.0 - bend * bend) * (GELU_A * (1.0 + 3.0 * GELU_B * square))
        slope = slope.astype(bf16)
        result = midway + b_down + jnp.dot(activ, w_down, preferred_element_type=f32)
        grad_low = to_chips(cotangent, activ).reshape(own, width)
        result = result.astype(bf16)

        grad_out = grad_low.astype(f32)
        d_down_b = jnp.sum(grad_out, axis=0, keepdims=True)

        def halves(a):
            a = a.reshape(F, 2, -1, a.shape[1])
            return pick(a, 1 - core, 1), pick(a, core, 1)

        def add(a, b):
            return (a.astype(f32) + b.astype(f32)).astype(bf16)

        d_down = dot(activ, grad_low, 0, 0).astype(bf16)
        give, keep = halves(d_down)
        d_down_other = swap(give)
        d_pre = (dot(after(grad_low, give), w_down, 1, 1) * slope.astype(f32)).astype(bf16)
        d_up = dot(hidden2, d_pre, 0, 0).astype(bf16)
        give_up, keep_up = halves(d_up)
        d_up_other = swap(give_up)
        d_hidden2 = dot(after(d_pre, give_up), w_up, 1, 1)
        d_up_b = jnp.sum(d_pre.astype(f32), axis=0, keepdims=True)
        d_norm2, d_gain2, d_shift2 = norm_backward(d_hidden2, xhat2, inverse2, gain2)
        d_mid = grad_out + d_norm2
        d_branch = d_mid.astype(bf16)
        d_mixed = dot(d_branch, w_out, 1, 1).astype(bf16)
        d_mixed_other = swap(lax.dynamic_slice_in_dim(d_mixed, (1 - core) * half, half, 1))
        d_out = dot(mixed_own, d_branch, 0, 0).astype(bf16)
        d_out_b = jnp.sum(d_branch.astype(f32), axis=0, keepdims=True)
        give_out, keep_out = halves(d_out)
        d_down_sum = add(keep, d_down_other).reshape(F, X, -1, width)
        d_second = jnp.concatenate(
            [
                add(keep_up, d_up_other).reshape(F, X, thin, hidden),
                add(keep_out, swap(give_out)).reshape(F, X, thin, width),
                fold(d_down_sum, thin),
            ],
            axis=3,
        )
        second_state = reduce_far(d_second.reshape(outer, inner, X, thin, -1), i, x)

        d_heads = in_order(lax.dynamic_slice_in_dim(d_mixed, core * half, half, 1), d_mixed_other, 0)
        d_heads = after(d_heads, *second_state[1])
        if chips == 1:
            dq, dk, dv = attend_back(q, k, v, d_heads, lse, seg_col, seg_row)
        else:
            dq, dk, dv = attend_far_back(q, k, v, d_heads, lse, allowed)
            dk, dv = (
                lax.psum_scatter(
                    t.astype(bf16), "fsdp", scatter_dimension=0, tiled=True, axis_index_groups=groups
                )
                for t in (dk, dv)
            )
            dq = dq.astype(bf16)
        output = to_blocks(result, dq)
        d_joined = jnp.concatenate([dq, dk, dv], axis=1)
        d_w_heads = dot(hidden1, d_joined, 0, 0)
        second_plane = reduce_sides(second_state, i, x, (), (dq,))
        d_hidden1 = dot(after(d_joined, second_plane), w_heads, 1, 1)
        d_hidden1_other = swap(lax.dynamic_slice_in_dim(d_hidden1, (1 - core) * own, own, 0).astype(bf16))
        d_hidden1 = lax.dynamic_slice_in_dim(d_hidden1, core * own, own, 0) + d_hidden1_other.astype(f32)
        xhat1, inverse1 = standardize(x_own)
        d_norm1, d_gain1, d_shift1 = norm_backward(d_hidden1, xhat1, inverse1, gain1)
        d_in = (d_mid + d_norm1).astype(bf16)
        d_inputs = to_blocks(d_in)
        d_second_red = reduce_line(second_plane, o, d_in)

        d_bias = jnp.sum(d_joined.astype(f32), axis=0, keepdims=True)

        d_small = pack_small(core, (d_out_b, d_gain1, d_shift1, d_down_b, d_gain2, d_shift2), d_bias, d_up_b)
        for axis, size in (("dp", dp_size), ("fsdp", F)):
            bit = 1
            while bit < size:
                d_small += lax.ppermute(d_small, axis, [(d, d ^ bit) for d in range(size)])
                bit *= 2
        d_first = d_w_heads.astype(bf16)
        first_state = reduce_far(d_first.reshape(outer, inner, X, slim, lanes), i, x)
        d_first_red = reduce_line(reduce_sides(first_state, i, x, (d_in,), ()), o)

        d_first_red, d_second_red = [gather_x(t, x) for t in (d_first_red, d_second_red)]
        first_o, second_o = [swap(t) for t in (d_first_red, d_second_red)]
        cols = half
        pieces = []
        for n in range(3):
            sl = slice(n * cols, (n + 1) * cols)
            pieces.append(in_order(d_first_red[:, sl], first_o[:, sl], 1))
        d_qkv_w = jnp.concatenate(pieces, axis=1).astype(f32)
        small_own = lax.dynamic_slice_in_dim(d_small[:8].reshape(8, F, part), f, 1, 1)
        vec = [small_own[n, 0] for n in range(8)]
        d_up_b = lax.dynamic_slice_in_dim(d_small[8:].reshape(hidden), f * deep, deep)
        d_second_w = in_order(d_second_red, second_o, 0).astype(f32)
        d_up_w, d_out_w = d_second_w[:, :hidden], d_second_w[:, hidden : hidden + width]
        d_down_w = jnp.stack(
            [
                d_second_w[:, at : at + width].reshape(2 * X, thin, width)
                for at in range(hidden + width, d_second_w.shape[1], width)
            ],
            axis=1,
        ).reshape(deep, width)
        return (
            output,
            d_inputs,
            d_qkv_w,
            vec[0],
            vec[1],
            d_out_w,
            vec[2],
            vec[3],
            vec[4],
            d_up_w,
            d_up_b,
            d_down_w,
            vec[5],
            vec[6],
            vec[7],
        )

    return local


def solution(mesh):
    in_specs = (
        P("dp", "fsdp", None),
        P("dp", "fsdp"),
        P("dp", "fsdp", None),
        P("fsdp", None),
        P("fsdp"),
        P("fsdp"),
        P("fsdp", None),
        P("fsdp"),
        P("fsdp"),
        P("fsdp"),
        P("fsdp", None),
        P("fsdp"),
        P("fsdp", None),
        P("fsdp"),
        P("fsdp"),
        P("fsdp"),
    )
    out_specs = (
        P("dp", "fsdp", None),
        P("dp", "fsdp", None),
        P("fsdp", None),
        P("fsdp"),
        P("fsdp"),
        P("fsdp", None),
        P("fsdp"),
        P("fsdp"),
        P("fsdp"),
        P("fsdp", None),
        P("fsdp"),
        P("fsdp", None),
        P("fsdp"),
        P("fsdp"),
        P("fsdp"),
    )
    local = build(mesh.shape["dp"], mesh.shape["fsdp"])
    return jax.shard_map(local, mesh=mesh, in_specs=in_specs, out_specs=out_specs, check_vma=False)
```
